32 devices in a mesh: seq: 8 (over z, y), head: 4 (over x, core).
Axes of the slice: x: 2, y: 2, z: 4, core: 2. Of those that a mesh axis runs over, the one named last changes fastest.
Arguments:
- mamba_inner: bfloat16 [1024, 3072], P('seq', 'head'), may hold values from -6 to 6
- mamba_groups: bfloat16 [1024, 512], P('seq'), may hold values from -6 to 6
- selective_gate: bfloat16 [1024, 3072], P('seq', 'head'), may hold values from -6 to 6
- step_raw: float32 [48, 1024], P('head', 'seq'), may hold values from -3 to 3
- step_bias: float32 [48], P('head'), may hold values from -0.5 to 0.5
- decay_log: float32 [48], P('head'), may hold values from -12 to -2
- conv_inner: float32 [4, 3072], P(None, 'head'), may hold values from -3 to 3
- conv_groups: float32 [4, 512], replicated, may hold values from -3 to 3
- gated_norm_gain: float32 [3072], P('head'), may hold values from 0.1 to 1.9
- query_rows: bfloat16 [1024, 1024], P('seq', 'head'), may hold values from -8 to 8
- key_rows: bfloat16 [1024, 256], P('seq'), may hold values from -8 to 8
- value_rows: bfloat16 [1024, 256], P('seq'), may hold values from -6 to 6
- segment_ids: int32 [1024], P('seq'), may hold values from 0 to 15, never falling along the last dimension, each value on 1 to 682 neighbouring positions
- mamba_proj: bfloat16 [3072, 2048], P('head'), may hold values from -0.109375 to 0.109375
- attn_proj: bfloat16 [1024, 2048], P('head'), may hold values from -0.1875 to 0.1875
Outputs:
- mixed: bfloat16 [1024, 2048], P('seq', 'head')
The draws below stay inside these ranges and needn't reach their ends.
Inputs may be any that keep to these rules, and one draw needn't show every extreme that they name: `segment_ids`: prompt numbers never fall along the tokens; each prompt holds 1 to 682 tokens and one holds exactly 682.
All inputs are finite; a program needn't handle non-finite values.
Results may differ from the reference program's by a relative error of at most 0.015.
Values may be sent and summed in bfloat16 or wider, within the bound.
A program may use at most 128 MiB of HBM per device.

```python
import math
import jax
import jax.numpy as jnp
import numpy as np
from jax import lax

D = 2048
MAMBA_HEADS = 48
HEAD_CHANNELS = 64
STATE_SIZE = 256
KCONV = 4
QH = 8
KVH = 2
HD = 128
BLOCK_TOKENS = 128
SEGS = 16
MAMBA_CHANNELS = 3072
PACKED_TOKENS = 1024
LONGEST = 682
N_SEQ = 8


def draw_decay_log(key, part):
    slow_share = 0.5
    slow = jax.random.uniform(jax.random.fold_in(key, 1), (MAMBA_HEADS,)) < slow_share
    slow_rate = jax.random.uniform(jax.random.fold_in(key, 2), (MAMBA_HEADS,), minval=0.3, maxval=1.5) / LONGEST
    fast_rate = jnp.exp(jax.random.uniform(jax.random.fold_in(key, 3), (MAMBA_HEADS,), minval=math.log(0.01), maxval=math.log(0.08)))
    return jnp.log(jnp.where(slow, slow_rate, fast_rate)).astype(jnp.float32)


def draw_step_raw(key, part):
    piece = max(BLOCK_TOKENS // 2, 1)
    pieces = (PACKED_TOKENS + piece - 1) // piece
    offsets = jax.random.uniform(jax.random.fold_in(key, 21), (MAMBA_HEADS, pieces), minval=-2.5, maxval=2.5)
    spread = jnp.repeat(offsets, piece, axis=1)[:, :PACKED_TOKENS]
    noise = jnp.clip(0.5 * jax.random.normal(jax.random.fold_in(key, 22), (MAMBA_HEADS, PACKED_TOKENS), jnp.float32), -1.5, 1.5)
    return jnp.clip(spread + noise, -3.0, 3.0).astype(jnp.float32)


def extreme_signs(key, salt, shape):
    return jnp.where(jax.random.bernoulli(jax.random.fold_in(key, salt), 0.5, shape), 8.0, -8.0).astype(jnp.float32)


def draw_key_rows(key, part):
    base = jnp.clip(jax.random.normal(jax.random.fold_in(key, 5), (PACKED_TOKENS, KVH * HD), jnp.float32), -6.0, 6.0)
    order = jnp.arange(PACKED_TOKENS)
    columns = jnp.arange(KVH * HD)
    heavy = (order % 257 == 11)[:, None] & (columns < HD)[None, :]
    base = jnp.where(heavy, extreme_signs(key, 31, (PACKED_TOKENS, KVH * HD)), base)
    return base.astype(jnp.bfloat16)


def draw_query_rows(key, part):
    base = jnp.clip(jax.random.normal(jax.random.fold_in(key, 9), (PACKED_TOKENS, QH * HD), jnp.float32), -6.0, 6.0)
    order = jnp.arange(PACKED_TOKENS)
    columns = jnp.arange(QH * HD)
    heavy = (order % 31 == 17)[:, None] & (columns < QH // KVH * HD)[None, :]
    base = jnp.where(heavy, extreme_signs(key, 33, (PACKED_TOKENS, QH * HD)), base)
    return base.astype(jnp.bfloat16)


def levels(stream_key, shape, cuts, smallest, largest):
    level = 1.0
    for axis_at, shards_of in cuts:
        draws = jax.random.uniform(jax.random.fold_in(jax.random.fold_in(stream_key, 6), axis_at), (shards_of,), jnp.float32, smallest / len(cuts), largest / len(cuts))
        level = level * jnp.repeat(jnp.exp(draws), shape[axis_at] // shards_of).reshape((-1,) + (1,) * (len(shape) - 1 - axis_at))
    return level


def length_profile(count, total, bound, skew):
    weights = [(1 << 20) // math.isqrt(grade ** skew) + 1 for grade in range(2, count + 1)]
    spare, holding = total - bound - (count - 1), [1] * (count - 1)
    while spare > 0:
        free = [i for i in range(count - 1) if holding[i] < bound]
        mass, budget = sum([weights[i] for i in free]), spare
        for i in free:
            extra = min(bound - holding[i], max(1, budget * weights[i] // mass), spare)
            holding[i] = holding[i] + extra
            spare = spare - extra
    return np.array([bound] + holding)


def ragged_sizes(own_key, count, total, most, slope):
    if count == 2:
        one = jax.random.randint(own_key, (), max(1, total - most), min(most, total - 1) + 1)
        return jnp.stack([one, total - one])
    sizes = jnp.asarray(length_profile(count, total, most, slope), jnp.int32)
    couples = (count - 1) // 2
    donor, taker = sizes[1:1 + 2 * couples:2], sizes[2:2 + 2 * couples:2]
    slack = jnp.minimum(donor - 1, most - taker)
    moved = jax.random.randint(jax.random.fold_in(own_key, 1), (couples,), 0, 1 << 20) % (slack + 1)
    sizes = sizes.at[1:1 + 2 * couples:2].set(donor - moved).at[2:2 + 2 * couples:2].set(taker + moved)
    return sizes[jax.random.permutation(jax.random.fold_in(own_key, 2), count)]


def gaussian(stream_key, shape, deviation, bound, shards=(), kind=jnp.bfloat16):
    factor_of = levels(stream_key, shape, shards, -0.22, 0.18) if shards else 1.0
    entries = jax.random.normal(stream_key, shape, jnp.float32) * deviation * factor_of
    return jnp.minimum(jnp.maximum(entries, -bound), bound).astype(kind)


def setup_inputs(seed: int = 0) -> dict:
    key_list = jax.random.split(jax.random.key(seed), 16)
    mamba_inner = gaussian(key_list[0], (PACKED_TOKENS, MAMBA_CHANNELS), 1.0, 6.0, ((0, 8), (1, 4)))
    mamba_groups = gaussian(key_list[1], (PACKED_TOKENS, 2 * STATE_SIZE), 1.0, 6.0, ((0, 8),))
    selective_gate = gaussian(key_list[2], (PACKED_TOKENS, MAMBA_CHANNELS), 1.0, 6.0, ((0, 8), (1, 4)))
    step_raw = draw_step_raw(jax.random.fold_in(key_list[15], 71), 0)
    step_bias = jnp.clip(jax.random.uniform(key_list[4], (MAMBA_HEADS,), jnp.float32, -0.5, 0.5) * levels(key_list[4], (MAMBA_HEADS,), ((0, 4),), -0.4, 0.0), -0.5, 0.5)
    decay_log = draw_decay_log(jax.random.fold_in(key_list[15], 71), 0)
    conv_inner = gaussian(key_list[6], (KCONV, MAMBA_CHANNELS), 0.5, 3.0, ((1, 4),), jnp.float32)
    conv_groups = gaussian(key_list[7], (KCONV, 2 * STATE_SIZE), 0.5, 3.0, (), jnp.float32)
    gated_norm_gain = jnp.clip(1.0 + 0.18 * jax.random.normal(key_list[8], (MAMBA_CHANNELS,), jnp.float32), 0.1, 1.9)
    query_rows = draw_query_rows(jax.random.fold_in(key_list[15], 71), 0)
    key_rows = draw_key_rows(jax.random.fold_in(key_list[15], 71), 0)
    value_rows = gaussian(key_list[11], (PACKED_TOKENS, KVH * HD), 1.0, 6.0, ((0, 8),))
    segment_ids = jnp.searchsorted(jnp.cumsum(ragged_sizes(key_list[12], SEGS, PACKED_TOKENS, LONGEST, 2)), jnp.arange(PACKED_TOKENS), side="right").astype(jnp.int32)
    mamba_proj = gaussian(key_list[13], (MAMBA_CHANNELS, D), MAMBA_CHANNELS ** -0.5, 0.109375, ((0, 4),))
    attn_proj = gaussian(key_list[14], (QH * HD, D), (QH * HD) ** -0.5, 0.1875, ((0, 4),))
    return {"mamba_inner": mamba_inner, "mamba_groups": mamba_groups, "selective_gate": selective_gate, "step_raw": step_raw, "step_bias": step_bias, "decay_log": decay_log, "conv_inner": conv_inner, "conv_groups": conv_groups, "gated_norm_gain": gated_norm_gain, "query_rows": query_rows, "key_rows": key_rows, "value_rows": value_rows, "segment_ids": segment_ids, "mamba_proj": mamba_proj, "attn_proj": attn_proj}


def conv_silu(rows, weight, segs, rim_rows, rim_segs):
    item_count = rows.shape[0]
    padded = jnp.concatenate([rim_rows.astype(jnp.float32), rows.astype(jnp.float32)], 0)
    seg_pad = jnp.concatenate([rim_segs, segs], 0)
    total = jnp.zeros(rows.shape, jnp.float32)
    for offset in range(weight.shape[0]):
        window = padded[offset:offset + item_count]
        keep = (seg_pad[offset:offset + item_count] == segs).astype(jnp.float32)
        total = total + weight[offset][None, :] * window * keep[:, None]
    return jax.nn.silu(total).astype(jnp.bfloat16)

def mamba_local(inner, groups, segs, steps, rates, prev_last):
    highest = lax.Precision.HIGHEST
    cumul = jnp.cumsum(-steps * rates[:, None], axis=1)
    read_b = groups[:, :STATE_SIZE]
    read_c = groups[:, STATE_SIZE:]
    intersection = jnp.dot(read_c, read_b.T, preferred_element_type=jnp.float32)
    order = jnp.arange(segs.shape[0], dtype=jnp.int32)
    live = (segs[:, None] == segs[None, :]) & (order[:, None] >= order[None, :])
    decays = jnp.exp(jnp.where(live[None], cumul[:, :, None] - cumul[:, None, :], -jnp.inf))
    mixing = intersection[None] * decays
    scaled = inner.astype(jnp.float32) * steps.T[:, :, None]
    output = jnp.einsum('htj,jhd->thd', mixing, scaled, precision=highest)
    tail = jnp.exp(cumul[:, -1:] - cumul) * (segs == segs[-1]).astype(jnp.float32)[None, :]
    local_state = jnp.einsum('ht,thd,tn->hdn', tail, scaled, read_b.astype(jnp.float32), precision=highest)
    through = jnp.exp(cumul[:, -1]) * (segs[-1] == prev_last).astype(jnp.float32)
    return (output, through, local_state, cumul)

def mamba_incoming(output, incoming, groups, segs, cumul, prev_last):
    read_c = groups[:, STATE_SIZE:].astype(jnp.float32)
    joined = (segs == prev_last).astype(jnp.float32)
    from_carry = jnp.einsum('hdn,tn->thd', incoming, read_c, precision=lax.Precision.HIGHEST)
    return output + jnp.exp(cumul).T[:, :, None] * joined[:, None, None] * from_carry

def reference(mamba_inner, mamba_groups, selective_gate, step_raw, step_bias, decay_log, conv_inner, conv_groups, gated_norm_gain, query_rows, key_rows, value_rows, segment_ids, mamba_proj, attn_proj):
    segs = segment_ids
    zero_segs = jnp.zeros((KCONV - 1,), jnp.int32)
    inner_filtered = conv_silu(mamba_inner, conv_inner, segs, jnp.zeros((KCONV - 1, MAMBA_CHANNELS), jnp.float32), zero_segs)
    groups_conv = conv_silu(mamba_groups, conv_groups, segs, jnp.zeros((KCONV - 1, 2 * STATE_SIZE), jnp.float32), zero_segs)
    steps = jax.nn.softplus(step_raw + step_bias[:, None])
    rates = jnp.exp(decay_log)
    inner_block_rows = inner_filtered.reshape(N_SEQ, BLOCK_TOKENS, MAMBA_HEADS, HEAD_CHANNELS)
    group_blocks = groups_conv.reshape(N_SEQ, BLOCK_TOKENS, 2 * STATE_SIZE)
    seg_blocks = segs.reshape(N_SEQ, BLOCK_TOKENS)
    step_blocks = steps.reshape(MAMBA_HEADS, N_SEQ, BLOCK_TOKENS).transpose(1, 0, 2)

    def advance(carry, block):
        state, prev_last = carry
        inner, groups, block_segs, block_steps = block
        output, through, local_state, cumul = mamba_local(inner, groups, block_segs, block_steps, rates, prev_last)
        output = mamba_incoming(output, state, groups, block_segs, cumul, prev_last)
        return ((through[:, None, None] * state + local_state, block_segs[-1]), output)
    initial_carry = (jnp.zeros((MAMBA_HEADS, HEAD_CHANNELS, STATE_SIZE), jnp.float32), jnp.zeros((), jnp.int32))
    final_carry, mixer_outputs = lax.scan(advance, initial_carry, (inner_block_rows, group_blocks, seg_blocks, step_blocks))
    selective_output = mixer_outputs.reshape(PACKED_TOKENS, MAMBA_HEADS, HEAD_CHANNELS)
    gated_values = selective_output * jax.nn.silu(selective_gate.astype(jnp.float32)).reshape(PACKED_TOKENS, MAMBA_HEADS, HEAD_CHANNELS)
    mean_square = lax.optimization_barrier(jnp.mean(gated_values * gated_values, axis=-1, keepdims=True))
    normalized_rows = (gated_values * lax.rsqrt(mean_square + 1e-05) * gated_norm_gain.reshape(MAMBA_HEADS, HEAD_CHANNELS)).astype(jnp.bfloat16).reshape(PACKED_TOKENS, MAMBA_CHANNELS)
    scale = 1.0 / math.sqrt(HD)
    query_blocks = query_rows.reshape(N_SEQ, BLOCK_TOKENS, KVH, QH // KVH, HD)
    keys_all = key_rows.reshape(PACKED_TOKENS, KVH, HD).astype(jnp.float32)
    values_all = value_rows.reshape(PACKED_TOKENS, KVH, HD).astype(jnp.float32)
    positions = jnp.arange(PACKED_TOKENS, dtype=jnp.int32)

    def attend(block):
        queries, index = block
        first = (index * BLOCK_TOKENS).astype(jnp.int32)
        query_pos = first + jnp.arange(BLOCK_TOKENS, dtype=jnp.int32)
        query_seg = lax.dynamic_slice_in_dim(segs, first, BLOCK_TOKENS)
        scores = jnp.einsum('tgrd,kgd->grtk', queries.astype(jnp.float32), keys_all) * scale
        allowed = (segs[None, :] == query_seg[:, None]) & (positions[None, :] <= query_pos[:, None])
        scores = jnp.where(allowed[None, None], scores, -jnp.inf)
        top = lax.optimization_barrier(jnp.max(scores, axis=-1, keepdims=True))
        weights = jnp.exp(scores - top)
        total = lax.optimization_barrier(jnp.sum(weights, axis=-1))
        rounded = lax.optimization_barrier(weights.astype(jnp.bfloat16))
        summed = jnp.einsum('grtk,kgd->tgrd', rounded.astype(jnp.float32), values_all)
        return (summed / total.transpose(2, 0, 1)[..., None]).astype(jnp.bfloat16)
    attended = lax.map(attend, (query_blocks, jnp.arange(N_SEQ, dtype=jnp.int32))).reshape(PACKED_TOKENS, QH * HD)
    terms = jnp.dot(normalized_rows, mamba_proj, preferred_element_type=jnp.float32) + jnp.dot(attended, attn_proj, preferred_element_type=jnp.float32)
    return terms.astype(jnp.bfloat16)
```

```python
import functools
import math

import jax
import jax.numpy as jnp
from jax import lax
from jax.experimental import pallas as pl
from jax.experimental.pallas import tpu as pltpu
from jax.sharding import PartitionSpec as P

HEAD_CHANNELS = 64
STATE_SIZE = 256
QH = 8
KVH = 2
HD = 128
LANES = 128
RIM = 16
PIECES = 4
F32 = jnp.float32
BF16 = jnp.bfloat16
MESH = pl.DeviceIdType.MESH


def dot(a, b, contract):
    return lax.dot_general(a, b, ((contract[:1], contract[1:]), ((), ())), preferred_element_type=F32)


def iota(shape, axis):
    return lax.broadcasted_iota(jnp.int32, shape, axis)


def column(row):
    n = row.shape[1]
    eye = iota((n, n), 0) == iota((n, n), 1)
    return jnp.sum(jnp.where(eye, jnp.broadcast_to(row, (n, n)), 0.0), axis=1, keepdims=True)


def thirds(a):
    high = a.astype(BF16).astype(F32)
    rest = a - high
    middle = rest.astype(BF16).astype(F32)
    return jnp.concatenate([high, middle, rest - middle], axis=0).astype(BF16)


def to_columns(rows):
    n = rows.shape[0]
    pick = (iota((3 * n, n), 0) % n == iota((3 * n, n), 1)).astype(BF16)
    return dot(thirds(rows), pick, (0, 0))


def kernel(
    n_seq,
    n_head,
    inner_hbm,
    groups_hbm,
    gate_hbm,
    step_hbm,
    bias_hbm,
    decay_hbm,
    taps_inner_hbm,
    taps_groups_hbm,
    gain_hbm,
    query_hbm,
    key_hbm,
    value_hbm,
    segs_hbm,
    mamba_proj_hbm,
    attn_proj_hbm,
    out_ref,
    segs_ref,
    step_in,
    bias_ref,
    decay_ref,
    taps_inner_ref,
    taps_groups_ref,
    gain_ref,
    query_ref,
    gate_ref,
    x_in,
    g_in,
    rim_x,
    rim_g,
    segt,
    kv,
    pad_x,
    pad_g,
    conv_x,
    conv_b,
    conv_c,
    y_ref,
    state,
    e_send,
    e_recv,
    f_send,
    f_recv,
    both,
    mproj,
    aproj,
    rs_send,
    rs_recv,
    top_ref,
    total_ref,
    summed_ref,
    ready,
    load_sem,
    weight_sem,
    x_ss,
    x_rs,
    g_ss,
    g_rs,
    step_sem,
    rim_ss,
    rim_rs,
    seg_ss,
    seg_rs,
    kv_ss,
    kv_rs,
    share_ss,
    share_rs,
    e_ss,
    e_rs,
    f_ss,
    f_rs,
    rs_ss,
    rs_rs,
):
    tokens, channels = gate_ref.shape
    heads = step_in.shape[1]
    half = channels // 2
    few = heads // 2
    chunks = half // LANES
    wide = groups_hbm.shape[1]
    taps = taps_inner_ref.shape[0]
    depth = STATE_SIZE // PIECES
    heads_here = query_ref.shape[1] // HD
    me = lax.axis_index("seq")
    mine = lax.axis_index("head")
    pair, side = me // 2, me % 2
    other = 1 - side
    last_pair = n_seq // 2 - 1
    partner = me + 1 - 2 * side
    upper = lax.min(me + 2, n_seq - 1)
    lower = lax.max(me - 2, 0)
    following = lax.min(me + 1, n_seq - 1)
    previous = lax.max(me - 1, 0)
    core = mine % 2
    sibling = mine + 1 - 2 * core
    opposite = (mine + 2) % n_head
    opposite_sibling = (sibling + 2) % n_head
    has_upper, has_lower = pair < last_pair, pair > 0

    def at_seq(s):
        return (s, mine)

    def at_head(h):
        return (me, h)

    def remote(src, dst, ss, rs, target):
        return pltpu.make_async_remote_copy(src, dst, ss, rs, device_id=target, device_id_type=MESH)

    def part(which, c):
        return pl.ds(pl.multiple_of(which * half + c * LANES, LANES), LANES)

    def side_half(which):
        return pl.ds(pl.multiple_of(which * half, LANES), half)

    core_cols = pl.ds(pl.multiple_of(core * STATE_SIZE, STATE_SIZE), STATE_SIZE)
    kv_head = mine * heads_here // (QH // KVH)
    kv_cols = pl.ds(pl.multiple_of(kv_head * HD, HD), HD)
    body = pl.ds(0, tokens)

    weights = [
        pltpu.make_async_copy(mamba_proj_hbm, mproj, weight_sem.at[0]),
        pltpu.make_async_copy(attn_proj_hbm, aproj, weight_sem.at[1]),
    ]
    loads = [
        pltpu.make_async_copy(src, dst, load_sem.at[i])
        for i, (src, dst) in enumerate(
            (
                (segs_hbm, segs_ref),
                (key_hbm.at[:, kv_cols], kv.at[me, 0, body]),
                (value_hbm.at[:, kv_cols], kv.at[me, 1, body]),
                (groups_hbm, g_in.at[side]),
                (taps_groups_hbm, taps_groups_ref),
                (inner_hbm.at[:, side_half(side)], x_in.at[side]),
                (taps_inner_hbm.at[:, side_half(side)], taps_inner_ref),
                (step_hbm, step_in.at[side]),
                (bias_hbm, bias_ref),
                (decay_hbm, decay_ref),
                (query_hbm, query_ref),
                (gate_hbm, gate_ref),
                (gain_hbm, gain_ref),
            )
        )
    ]

    barrier = pltpu.get_barrier_semaphore()

    def hello(target):
        pl.semaphore_signal(barrier, inc=1, device_id=target, device_id_type=MESH)

    hello(at_seq(partner))
    hello(at_head(sibling))
    hello(at_head(opposite))

    def hello_later(k, _):
        hello(at_seq(k))
        return 0

    lax.fori_loop(2 * pair + 2, n_seq, hello_later, 0)
    for w in loads:
        w.start()
    pl.semaphore_wait(barrier, 3 + 2 * pair)

    def answer(k, _):
        pl.semaphore_signal(ready.at[me], inc=1, device_id=at_seq(k), device_id_type=MESH)
        return 0

    lax.fori_loop(0, 2 * pair, answer, 0)

    tail_rows = pl.ds(tokens - RIM, RIM)

    def rim_copies(kind, target, slot, which):
        return [
            remote(
                inner_hbm.at[tail_rows, side_half(which)], rim_x.at[slot], rim_ss.at[kind, 0], rim_rs.at[slot, 0], at_seq(target)
            ),
            remote(groups_hbm.at[tail_rows, :], rim_g.at[slot], rim_ss.at[kind, 1], rim_rs.at[slot, 1], at_seq(target)),
        ]

    def rim_next():
        return rim_copies(0, following, other, other)

    def rim_skip():
        return rim_copies(1, upper, 0, side)

    def group_copy(block):
        return remote(
            groups_hbm.at[:, core_cols], g_in.at[block, :, core_cols], g_ss.at[0], g_rs.at[0], at_seq(partner)
        )

    def group_share():
        return remote(
            g_in.at[other, :, core_cols], g_in.at[other, :, core_cols], g_ss.at[1], g_rs.at[1], at_head(sibling)
        )

    def x_copy(block, c):
        return remote(
            inner_hbm.at[:, part(other, c)],
            x_in.at[block, :, pl.ds(c * LANES, LANES)],
            x_ss.at[c],
            x_rs.at[c],
            at_seq(partner),
        )

    def step_copy(block):
        return remote(step_hbm, step_in.at[block], step_sem.at[0], step_sem.at[1], at_seq(partner))

    loads[0].wait()
    own_segs = jnp.broadcast_to(segs_ref[...].reshape(1, tokens).astype(F32), (RIM, tokens)).astype(BF16)
    segt[1 + side] = own_segs

    def seg_copy(kind, target, src, dst):
        return remote(segt.at[src], segt.at[dst], seg_ss.at[kind], seg_rs.at[dst], at_seq(target))

    step_copy(side).start()
    seg_copy(0, partner, 1 + side, 1 + side).start()

    @pl.when(side == 0)
    def _():
        for c in rim_next():
            c.start()

    group_copy(side).start()
    for c in range(chunks):
        x_copy(side, c).start()

    def kv_copy(b, k):
        return remote(kv.at[b, core], kv.at[b, core], kv_ss.at[k], kv_rs.at[b], at_seq(k))

    def kv_share(b):
        return remote(kv.at[b, core], kv.at[b, core], share_ss.at[b], share_rs.at[b], at_head(sibling))

    def pass_on(d, _):
        kv_copy(me - d, partner).wait_recv()
        kv_share(me - d).start()
        return 0

    def conv_flags(b, before):
        now = segt[b + 1].astype(F32)[0:8]
        both_blocks = jnp.concatenate([before, now], axis=1)
        row = iota((8, tokens), 0)
        flags = now
        for back in range(1, taps):
            kept = (pltpu.roll(both_blocks, back, 1)[:, tokens:] == now).astype(F32)
            flags = jnp.where(row == back, kept, flags)
        eye = (iota((8, 8), 0) == iota((8, 8), 1)).astype(BF16)
        return dot(flags.astype(BF16), eye, (0, 0))

    def keeps_of(flags, n):
        return [jnp.broadcast_to(flags[:n, back : back + 1], (n, LANES)) > 0.5 for back in range(taps - 1, 0, -1)]

    def conv(pad, b, cols, keeps, weight_ref, n):
        acc = weight_ref[taps - 1 : taps, cols] * pad[b, RIM : RIM + n, cols]
        for k in range(taps - 1):
            first = RIM - (taps - 1) + k
            term = weight_ref[k : k + 1, cols] * pad[b, first : first + n, cols]
            acc = acc + jnp.where(keeps[k], term, 0.0)
        return jax.nn.silu(acc).astype(BF16)

    def conv_groups(b, keeps, n):
        for out, base in ((conv_b, 0), (conv_c, STATE_SIZE)):
            for c in range(0, STATE_SIZE, LANES):
                at = slice(base + c, base + c + LANES)
                out[b, 0:n, c : c + LANES] = conv(pad_g, b, at, keeps, taps_groups_ref, n)

    def conv_inner(b, c, keeps, n):
        at = slice(c * LANES, (c + 1) * LANES)
        conv_x[b, 0:n, at] = conv(pad_x, b, at, keeps, taps_inner_ref, n)

    def rim_arrived(slot):
        for c in rim_copies(0, partner, slot, slot):
            c.wait_recv()

    for w in loads[3:7]:
        w.wait()
    pad_g[side, 0:RIM, :] = jnp.zeros((RIM, wide), F32)
    pad_x[side, 0:RIM, :] = jnp.zeros((RIM, half), F32)
    pad_g[side, RIM:, :] = g_in[side].astype(F32)
    pad_x[side, RIM:, :] = x_in[side].astype(F32)
    own_flags = conv_flags(side, jnp.full((8, tokens), -1.0, F32))
    own_keeps = keeps_of(own_flags, tokens)
    conv_groups(side, own_keeps, tokens)

    kv[me, 0, pl.ds(tokens, RIM), :] = own_segs
    kv[me, 1, pl.ds(tokens, RIM), :] = own_segs
    loads[1].wait()
    loads[2].wait()

    @pl.when(side == 0)
    def _():
        kv_copy(me, partner).start()

    @pl.when(has_upper)
    def _():
        pl.semaphore_wait(ready.at[upper], 1)

    @pl.when(has_upper & (side == 1))
    def _():
        pl.semaphore_wait(ready.at[following], 1)
        seg_copy(1, following, 2, 0).start()
        seg_copy(2, upper, 2, 0).start()
        for c in rim_skip():
            c.start()
        for c in rim_next():
            c.start()
        kv_copy(me, following).start()

    @pl.when(has_upper)
    def _():
        kv_copy(me, upper).start()

    for c in range(chunks):
        conv_inner(side, c, own_keeps, tokens)

    for w in loads[7:10]:
        w.wait()
    step_copy(other).wait_recv()
    seg_copy(0, partner, 1 + other, 1 + other).wait_recv()
    bias = column(bias_ref[...].reshape(1, heads))
    rates = jnp.exp(column(decay_ref[...].reshape(1, heads)))
    on_left = side == 0

    def mine_of(a):
        kept = jnp.where(on_left, a[:few], a[few:])
        return jnp.concatenate([kept, jnp.zeros((8 - few, a.shape[1]), F32)], axis=0)

    raw = mine_of(jnp.concatenate([step_in[0], step_in[1]], axis=1) + bias)
    steps = jnp.maximum(raw, 0.0) + jnp.log1p(jnp.exp(-jnp.abs(raw)))
    span = 2 * tokens
    row_t, col_t = iota((span, span), 0), iota((span, span), 1)
    upto = (row_t <= col_t).astype(BF16)
    sums = dot(thirds(-steps * mine_of(rates)), upto, (1, 0))
    cumul = sums[0:8] + sums[8:16] + sums[16:24]
    total = cumul[:, span - 1 : span]
    segs_rows8 = jnp.concatenate([segt[1].astype(F32)[0:8], segt[2].astype(F32)[0:8]], axis=1)
    last_seg = segs_rows8[:, span - 1 : span]
    weigh = jnp.where(segs_rows8 == last_seg, jnp.exp(total - cumul), 0.0) * steps
    cols = to_columns(jnp.concatenate([cumul, weigh, jnp.exp(cumul), segs_rows8], axis=0))
    left = iota((span, LANES), 1) < HEAD_CHANNELS

    def two_heads(base, c):
        a, b = base + 2 * c, base + 2 * c + 1
        return jnp.where(left, cols[:, a : a + 1], cols[:, b : b + 1])

    group_copy(other).wait_recv()
    group_share().start()

    @pl.when(has_lower)
    def _():
        seg_copy(0, partner, 0, 0).wait_recv()
        rim_arrived(0)

    @pl.when(pair == 0)
    def _():
        segt[0] = jnp.full((RIM, tokens), -1.0, BF16)
        rim_x[0] = jnp.zeros_like(rim_x[0])
        rim_g[0] = jnp.zeros_like(rim_g[0])

    @pl.when(side == 1)
    def _():
        rim_arrived(1)

    @pl.when(side == 0)
    def _():
        rim_x[1] = x_in[0, tokens - RIM :, :]
        rim_g[1] = g_in[0, tokens - RIM :, :]

    for b in range(2):
        pad_g[b, 0:RIM, :] = rim_g[b].astype(F32)
        pad_x[b, 0:RIM, :] = rim_x[b].astype(F32)
    first_keeps = keeps_of(conv_flags(side, segt[side].astype(F32)[0:8]), RIM)
    conv_groups(side, first_keeps, RIM)
    for c in range(chunks):
        conv_inner(side, c, first_keeps, RIM)
    prev_last = segt[0].astype(F32)[0:8, tokens - 1 : tokens]
    spread = iota((8, half), 1) // HEAD_CHANNELS == iota((8, half), 0)
    crossing_pair = jnp.where(last_seg == prev_last, jnp.exp(total), 0.0)
    through = jnp.sum(jnp.where(spread, crossing_pair, 0.0), axis=0, keepdims=True)
    joined = cols[:, 24:25] == prev_last[0:1]

    def send_far(k, _):
        pl.semaphore_wait(ready.at[k], 1)
        kv_copy(me, k).start()
        return 0

    lax.fori_loop(me + 3, n_seq, send_far, 0)

    other_keeps = keeps_of(conv_flags(other, segt[other].astype(F32)[0:8]), tokens)
    group_share().wait_recv()
    pad_g[other, RIM:, :] = g_in[other].astype(F32)
    conv_groups(other, other_keeps, tokens)
    read_b = conv_b[...].reshape(span, STATE_SIZE)
    read_c = conv_c[...].reshape(span, STATE_SIZE)

    def hop(src, dst, ss, rs, c, target):
        return remote(src.at[c], dst.at[c], ss.at[c], rs.at[c], at_seq(target))

    def e_hop(i, target):
        return hop(e_send, e_recv, e_ss, e_rs, i, target)

    for c in range(chunks):
        x_copy(other, c).wait_recv()
        lanes = slice(c * LANES, (c + 1) * LANES)
        pad_x[other, RIM:, lanes] = x_in[other, :, lanes].astype(F32)
        conv_inner(other, c, other_keeps, tokens)
        x = conv_x[:, :, lanes].reshape(span, LANES).astype(F32)
        state[:, lanes] = dot(read_b, (two_heads(8, c) * x).astype(BF16), (0, 0))

        @pl.when(pair == 0)
        def _():
            for r in range(PIECES):
                i = PIECES * c + r
                e_send[i] = state[r * depth : (r + 1) * depth, lanes].astype(BF16)
                e_hop(i, upper).start()

    for w in weights:
        w.start()

    for w in loads[10:]:
        w.wait()
    scale = 1.0 / math.sqrt(HD)
    queries = jnp.concatenate([query_ref[:, h * HD : (h + 1) * HD] for h in range(heads_here)], axis=0)
    rows = heads_here * tokens
    segs_q = jnp.concatenate([own_flags[:, 0:1]] * heads_here, axis=0)
    token_q = jnp.concatenate([iota((tokens, 1), 0)] * heads_here, axis=0)
    top_ref[...] = jnp.full((rows, 1), -1e30, F32)
    total_ref[...] = jnp.zeros((rows, 1), F32)
    summed_ref[...] = jnp.zeros((rows, HD), F32)

    def attend(d, _):
        k = me - d

        @pl.when(d > 0)
        def _():
            kv_share(k).wait_recv()

        scores = dot(queries, kv[k, 0, 0:tokens, :], (1, 1)) * scale
        segs_k = kv[k, 0, tokens:, :].astype(F32)[0:1, :tokens]
        allowed = (segs_k == segs_q) & (iota((rows, tokens), 1) + (k - me) * tokens <= token_q)
        scores = jnp.where(allowed, scores, -jnp.inf)
        top = top_ref[...]
        new_top = jnp.maximum(top, jnp.max(scores, axis=1, keepdims=True))
        rescale = jnp.exp(top - new_top)
        w = jnp.exp(scores - new_top)
        top_ref[...] = new_top
        total_ref[...] = total_ref[...] * rescale + jnp.sum(w, axis=1, keepdims=True)
        summed_ref[...] = summed_ref[...] * rescale + dot(w.astype(BF16), kv[k, 1, 0:tokens, :], (1, 0))
        return 0

    same_head = (iota((2 * LANES, LANES), 0) % LANES // HEAD_CHANNELS == iota((2 * LANES, LANES), 1) // HEAD_CHANNELS).astype(
        BF16
    )
    gain_row = gain_ref[...].reshape(1, channels)
    gains = [
        jnp.where(on_left, gain_row[:, :half], gain_row[:, half:]),
        jnp.where(on_left, gain_row[:, half:], gain_row[:, :half]),
    ]

    def norm(which, c, gain, y):
        at = part(which, c)
        gated = y * jax.nn.silu(gate_ref[:, at].astype(F32))
        square = gated * gated
        high = square.astype(BF16)
        parts = jnp.concatenate([high, (square - high.astype(F32)).astype(BF16)], axis=1)
        mean_square = dot(parts, same_head, (1, 0)) * (1.0 / HEAD_CHANNELS)
        normed = gated * lax.rsqrt(mean_square + 1e-05) * gain[:, c * LANES : (c + 1) * LANES]
        both[:, at] = normed.astype(BF16)

    def f_hop(c):
        return hop(f_send, f_recv, f_ss, f_rs, c, partner)

    @pl.when(pair == 0)
    def _():
        e_recv[...] = jnp.zeros_like(e_recv)

    live = (cols[:, 24:25] == segs_rows8[0:1]) & (row_t >= col_t)
    crossing = dot(read_c, read_b, (1, 1))
    for c in range(chunks):
        lanes = slice(c * LANES, (c + 1) * LANES)
        x = conv_x[:, :, lanes].reshape(span, LANES)
        got = []
        for h in (2 * c, 2 * c + 1):
            halves = []
            for rows_of, width in ((slice(0, tokens), tokens), (slice(tokens, span), span)):
                gap = cols[rows_of, h : h + 1] - cumul[h : h + 1, :width]
                decays = jnp.exp(jnp.where(live[rows_of, :width], gap, -jnp.inf))
                mixing = (crossing[rows_of, :width] * decays * steps[h : h + 1, :width]).astype(BF16)
                halves.append(dot(mixing, x[:width], (1, 0)))
            got.append(jnp.concatenate(halves, axis=0))
        y_ref[:, lanes] = jnp.where(left, got[0], got[1])

    def attention():
        lax.fori_loop(1, me + 1, pass_on, 0)
        lax.fori_loop(0, me + 1, attend, 0)
        attended = (summed_ref[...] / total_ref[...]).astype(BF16)
        for h in range(heads_here):
            both[:, channels + h * HD : channels + (h + 1) * HD] = attended[h * tokens : (h + 1) * tokens]

    pl.when(me >= n_seq // 2)(attention)
    for c in range(chunks):
        lanes = slice(c * LANES, (c + 1) * LANES)

        @pl.when(has_lower)
        def _():
            for r in range(PIECES):
                i = PIECES * c + r
                e_hop(i, partner).wait_recv()

                @pl.when(has_upper)
                def _():
                    enters = e_recv[i].astype(F32)
                    e_send[i] = (through[:, lanes] * enters + state[r * depth : (r + 1) * depth, lanes]).astype(BF16)
                    e_hop(i, upper).start()

        enters = jnp.concatenate([e_recv[PIECES * c + r] for r in range(PIECES)], axis=0)
        carried = jnp.where(joined, two_heads(16, c), 0.0) * dot(read_c, enters, (1, 0))
        y = y_ref[:, lanes] + carried
        f_send[c] = jnp.where(on_left, y[tokens:], y[:tokens]).astype(BF16)
        f_hop(c).start()
        norm(side, c, gains[0], jnp.where(on_left, y[:tokens], y[tokens:]))

    pl.when(me < n_seq // 2)(attention)
    for c in range(chunks):
        f_hop(c).wait_recv()
        norm(other, c, gains[1], f_recv[c].astype(F32))

    for w in weights:
        w.wait()
    width = out_ref.shape[1]

    def product(j, part_of):
        at = pl.ds(pl.multiple_of(j * width + part_of * (width // 2), LANES), width // 2)
        return dot(both[:, :channels], mproj[:, at], (1, 0)) + dot(both[:, channels:], aproj[:, at], (1, 0))

    def rs_copy(i, target):
        return remote(rs_send.at[i], rs_recv.at[i], rs_ss.at[i], rs_rs.at[i], at_head(target))

    to_pair = [rs_copy(h, sibling) for h in range(2)]
    to_sibling = [rs_copy(2 + h, sibling) for h in range(2)]
    to_opposite = [rs_copy(4 + h, opposite) for h in range(2)]
    for h in range(2):
        rs_send[h] = product(opposite_sibling, h).astype(BF16)
        to_pair[h].start()
    for h in range(2):
        away = product(opposite, h)
        to_pair[h].wait_recv()
        rs_send[4 + h] = (away + rs_recv[h].astype(F32)).astype(BF16)
        to_opposite[h].start()
    for h in range(2):
        rs_send[2 + h] = product(sibling, h).astype(BF16)
        to_sibling[h].start()
    for h in range(2):
        result = product(mine, h)
        to_sibling[h].wait_recv()
        result = result + rs_recv[2 + h].astype(F32)
        to_opposite[h].wait_recv()
        out_ref[:, h * (width // 2) : (h + 1) * (width // 2)] = (result + rs_recv[4 + h].astype(F32)).astype(BF16)

    for copy in (*to_pair, *to_sibling, *to_opposite, group_copy(side), group_share(), step_copy(side)):
        copy.wait_send()
    for c in range(chunks):
        x_copy(side, c).wait_send()
        f_hop(c).wait_send()
    seg_copy(0, partner, 1 + side, 1 + side).wait_send()

    @pl.when(me < n_seq - 1)
    def _():
        for c in rim_next():
            c.wait_send()

    @pl.when(has_upper & (side == 1))
    def _():
        for c in rim_skip():
            c.wait_send()
        seg_copy(1, following, 2, 0).wait_send()
        seg_copy(2, upper, 2, 0).wait_send()

    @pl.when(has_upper)
    def _():
        for i in range(PIECES * chunks):
            e_hop(i, upper).wait_send()

    def sent_kv(k, _):
        kv_copy(me, k).wait_send()
        return 0

    lax.fori_loop(me + 1, n_seq, sent_kv, 0)

    def sent_share(d, _):
        kv_share(me - d).wait_send()
        return 0

    lax.fori_loop(1, me + 1, sent_share, 0)


def shards(n_seq, n_head, *arrays):
    (inner, groups, gate, step, bias, decay, taps_i, taps_g, gain, query, key, value, segs, mproj, aproj) = arrays
    tokens, channels = inner.shape
    half = channels // 2
    wide = groups.shape[1]
    out_width = mproj.shape[1] // n_head
    chunks = half // LANES
    vmem = pl.BlockSpec(memory_space=pltpu.VMEM)
    hbm = pl.BlockSpec(memory_space=pltpu.HBM)
    dma = pltpu.SemaphoreType.DMA
    scratch = [
        pltpu.VMEM(segs.shape, segs.dtype),
        pltpu.VMEM((2, *step.shape), F32),
        pltpu.VMEM(bias.shape, F32),
        pltpu.VMEM(decay.shape, F32),
        pltpu.VMEM((taps_i.shape[0], half), F32),
        pltpu.VMEM(taps_g.shape, F32),
        pltpu.VMEM(gain.shape, F32),
        pltpu.VMEM(query.shape, BF16),
        pltpu.VMEM(gate.shape, BF16),
        pltpu.VMEM((2, tokens, half), BF16),
        pltpu.VMEM((2, tokens, wide), BF16),
        pltpu.VMEM((2, RIM, half), BF16),
        pltpu.VMEM((2, RIM, wide), BF16),
        pltpu.VMEM((3, RIM, tokens), BF16),
        pltpu.VMEM((n_seq, 2, tokens + RIM, HD), BF16),
        pltpu.VMEM((2, RIM + tokens, half), F32),
        pltpu.VMEM((2, RIM + tokens, wide), F32),
        pltpu.VMEM((2, tokens, half), BF16),
        pltpu.VMEM((2, tokens, STATE_SIZE), BF16),
        pltpu.VMEM((2, tokens, STATE_SIZE), BF16),
        pltpu.VMEM((2 * tokens, half), F32),
        pltpu.VMEM((STATE_SIZE, half), F32),
        *[pltpu.VMEM((PIECES * chunks, STATE_SIZE // PIECES, LANES), BF16) for _ in range(2)],
        *[pltpu.VMEM((chunks, tokens, LANES), BF16) for _ in range(2)],
        pltpu.VMEM((tokens, channels + query.shape[1]), BF16),
        pltpu.VMEM(mproj.shape, BF16),
        pltpu.VMEM(aproj.shape, BF16),
        pltpu.VMEM((6, tokens, out_width // 2), BF16),
        pltpu.VMEM((6, tokens, out_width // 2), BF16),
        *[pltpu.VMEM((query.shape[1] // HD * tokens, n), F32) for n in (1, 1, HD)],
        pltpu.SemaphoreType.REGULAR((n_seq,)),
        dma((13,)),
        dma((2,)),
        dma((chunks,)),
        dma((chunks,)),
        dma((2,)),
        dma((2,)),
        dma((2,)),
        dma((2, 2)),
        dma((2, 2)),
        dma((3,)),
        dma((3,)),
        *[dma((n_seq,)) for _ in range(4)],
        *[dma((PIECES * chunks,)) for _ in range(2)],
        *[dma((chunks,)) for _ in range(2)],
        dma((6,)),
        dma((6,)),
    ]
    return pl.pallas_call(
        functools.partial(kernel, n_seq, n_head),
        out_shape=jax.ShapeDtypeStruct((tokens, out_width), BF16),
        in_specs=[hbm] * 15,
        out_specs=vmem,
        scratch_shapes=scratch,
        compiler_params=pltpu.CompilerParams(
            collective_id=0, has_side_effects=True, vmem_limit_bytes=64 * 2**20
        ),
        name="mixer",
    )(*arrays)


def solution(mesh):
    placed = (
        P("seq", "head"),
        P("seq", None),
        P("seq", "head"),
        P("head", "seq"),
        P("head"),
        P("head"),
        P(None, "head"),
        P(),
        P("head"),
        P("seq", "head"),
        P("seq", None),
        P("seq", None),
        P("seq"),
        P("head", None),
        P("head", None),
    )
    return jax.shard_map(
        functools.partial(shards, mesh.shape["seq"], mesh.shape["head"]),
        mesh=mesh,
        in_specs=placed,
        out_specs=P("seq", "head"),
        check_vma=False,
    )
```

```python
import functools
import math

import jax
import jax.numpy as jnp
from jax import lax
from jax.experimental import pallas as pl
from jax.experimental.pallas import tpu as pltpu
from jax.sharding import PartitionSpec as P

HEAD_CHANNELS = 64
STATE_SIZE = 256
QH = 8
KVH = 2
HD = 128
LANES = 128
RIM = 16
PIECES = 4
F32 = jnp.float32
BF16 = jnp.bfloat16
MESH = pl.DeviceIdType.MESH


def dot(a, b, contract):
    return lax.dot_general(a, b, ((contract[:1], contract[1:]), ((), ())), preferred_element_type=F32)


def iota(shape, axis):
    return lax.broadcasted_iota(jnp.int32, shape, axis)


def column(row):
    n = row.shape[1]
    eye = iota((n, n), 0) == iota((n, n), 1)
    return jnp.sum(jnp.where(eye, jnp.broadcast_to(row, (n, n)), 0.0), axis=1, keepdims=True)


def thirds(a):
    high = a.astype(BF16).astype(F32)
    rest = a - high
    middle = rest.astype(BF16).astype(F32)
    return jnp.concatenate([high, middle, rest - middle], axis=0).astype(BF16)


def to_columns(rows):
    n = rows.shape[0]
    pick = (iota((3 * n, n), 0) % n == iota((3 * n, n), 1)).astype(BF16)
    return dot(thirds(rows), pick, (0, 0))


def kernel(
    n_seq,
    n_head,
    inner_hbm,
    groups_hbm,
    gate_hbm,
    step_hbm,
    bias_hbm,
    decay_hbm,
    taps_inner_hbm,
    taps_groups_hbm,
    gain_hbm,
    query_hbm,
    key_hbm,
    value_hbm,
    segs_hbm,
    mamba_proj_hbm,
    attn_proj_hbm,
    out_ref,
    segs_ref,
    step_in,
    bias_ref,
    decay_ref,
    taps_inner_ref,
    taps_groups_ref,
    gain_ref,
    query_ref,
    gate_ref,
    x_in,
    g_in,
    rim_x,
    rim_g,
    kv,
    pad_x,
    pad_g,
    conv_x,
    conv_b,
    conv_c,
    y_ref,
    state,
    e_send,
    e_recv,
    f_send,
    f_recv,
    both,
    mproj,
    aproj,
    rs_send,
    rs_recv,
    top_ref,
    total_ref,
    summed_ref,
    ready,
    load_sem,
    weight_sem,
    x_ss,
    x_rs,
    g_ss,
    g_rs,
    step_sem,
    rim_ss,
    rim_rs,
    seg_ss,
    seg_rs,
    kv_ss,
    across_ss,
    kv_rs,
    share_ss,
    share_rs,
    e_ss,
    e_rs,
    f_ss,
    f_rs,
    rs_ss,
    rs_rs,
):
    tokens, channels = gate_ref.shape
    heads = step_in.shape[1]
    half = channels // 2
    few = heads // 2
    chunks = half // LANES
    wide = groups_hbm.shape[1]
    taps = taps_inner_ref.shape[0]
    depth = STATE_SIZE // PIECES
    heads_here = query_ref.shape[1] // HD
    me = lax.axis_index("seq")
    mine = lax.axis_index("head")
    pair, side = me // 2, me % 2
    other = 1 - side
    last_pair = n_seq // 2 - 1
    partner = me + 1 - 2 * side
    upper = lax.min(me + 2, n_seq - 1)
    lower = lax.max(me - 2, 0)
    following = lax.min(me + 1, n_seq - 1)
    previous = lax.max(me - 1, 0)
    core = mine % 2
    sibling = mine + 1 - 2 * core
    opposite = (mine + 2) % n_head
    opposite_sibling = (sibling + 2) % n_head
    has_upper, has_lower = pair < last_pair, pair > 0

    def at_seq(s):
        return (s, mine)

    def at_head(h):
        return (me, h)

    def remote(src, dst, ss, rs, target):
        return pltpu.make_async_remote_copy(src, dst, ss, rs, device_id=target, device_id_type=MESH)

    def part(which, c):
        return pl.ds(pl.multiple_of(which * half + c * LANES, LANES), LANES)

    def side_half(which):
        return pl.ds(pl.multiple_of(which * half, LANES), half)

    def core_cols(kind):
        return pl.ds(pl.multiple_of(kind * STATE_SIZE + core * LANES, LANES), LANES)

    kv_head = mine * heads_here // (QH // KVH)
    kv_cols = pl.ds(pl.multiple_of(kv_head * HD, HD), HD)
    body = pl.ds(0, tokens)

    weights = [
        pltpu.make_async_copy(mamba_proj_hbm, mproj, weight_sem.at[0]),
        pltpu.make_async_copy(attn_proj_hbm, aproj, weight_sem.at[1]),
    ]
    loads = [
        pltpu.make_async_copy(src, dst, load_sem.at[i])
        for i, (src, dst) in enumerate(
            (
                (segs_hbm, segs_ref.at[1 + side, 0]),
                (key_hbm.at[:, kv_cols], kv.at[me, 0, body]),
                (value_hbm.at[:, kv_cols], kv.at[me, 1, body]),
                (groups_hbm, g_in.at[side]),
                (taps_groups_hbm, taps_groups_ref),
                (inner_hbm.at[:, side_half(side)], x_in.at[side]),
                (taps_inner_hbm.at[:, side_half(side)], taps_inner_ref),
                (step_hbm, step_in.at[side]),
                (bias_hbm, bias_ref),
                (decay_hbm, decay_ref),
                (query_hbm, query_ref),
                (gate_hbm, gate_ref),
                (gain_hbm, gain_ref),
            )
        )
    ]

    barrier = pltpu.get_barrier_semaphore()

    def hello(target):
        pl.semaphore_signal(barrier, inc=1, device_id=target, device_id_type=MESH)

    hello(at_seq(partner))
    hello(at_head(sibling))
    hello(at_head(opposite))

    def hello_later(s, _):
        hello(at_seq(me + 2 * s))
        return 0

    lax.fori_loop(1, last_pair - pair + 1, hello_later, 0)

    @pl.when(has_upper & (side == 1))
    def _():
        hello(at_seq(following))

    for w in loads:
        w.start()
    pl.semaphore_wait(barrier, 3 + pair + jnp.where(has_lower, other, 0))

    def answer(k):
        pl.semaphore_signal(ready.at[me], inc=1, device_id=at_seq(k), device_id_type=MESH)

    @pl.when(has_lower & (side == 0))
    def _():
        answer(previous)

    lax.fori_loop(1, pair + 1, lambda s, _: answer(me - 2 * s) or 0, 0)

    tail_rows = pl.ds(tokens - RIM, RIM)

    def rim_copies(kind, target, slot, which):
        return [
            remote(
                inner_hbm.at[tail_rows, side_half(which)], rim_x.at[slot], rim_ss.at[kind, 0], rim_rs.at[slot, 0], at_seq(target)
            ),
            remote(groups_hbm.at[tail_rows, :], rim_g.at[slot], rim_ss.at[kind, 1], rim_rs.at[slot, 1], at_seq(target)),
        ]

    def rim_next():
        return rim_copies(0, following, other, other)

    def rim_skip():
        return rim_copies(1, upper, 0, side)

    def group_copy(block, kind):
        at = core_cols(kind)
        return remote(groups_hbm.at[:, at], g_in.at[block, :, at], g_ss.at[kind], g_rs.at[kind], at_seq(partner))

    def group_share(kind):
        at = core_cols(kind)
        return remote(g_in.at[other, :, at], g_in.at[other, :, at], g_ss.at[2 + kind], g_rs.at[2 + kind], at_head(sibling))

    def x_copy(block, c):
        return remote(
            inner_hbm.at[:, part(other, c)],
            x_in.at[block, :, pl.ds(c * LANES, LANES)],
            x_ss.at[c],
            x_rs.at[c],
            at_seq(partner),
        )

    def step_copy(block):
        return remote(step_hbm, step_in.at[block], step_sem.at[0], step_sem.at[1], at_seq(partner))

    def seg_copy(kind, target, dst):
        return remote(segs_hbm, segs_ref.at[dst, 0], seg_ss.at[kind], seg_rs.at[dst], at_seq(target))

    step_copy(side).start()
    seg_copy(0, partner, 1 + side).start()

    group_copy(side, 0).start()
    x_copy(side, 0).start()

    @pl.when(side == 0)
    def _():
        for c in rim_next():
            c.start()

    for c in range(1, chunks):
        x_copy(side, c).start()
    group_copy(side, 1).start()

    def kv_copy(b, k):
        return remote(kv.at[b, core], kv.at[b, core], kv_ss.at[k], kv_rs.at[b], at_seq(k))

    def kv_share(b):
        return remote(kv.at[b, core], kv.at[b, core], share_ss.at[b], share_rs.at[b], at_head(sibling))

    def kv_across(b):
        return remote(kv.at[b, core], kv.at[b, core], across_ss.at[b], kv_rs.at[b], at_seq(partner))

    def pass_on(s, _):
        kv_copy(me - 2 * s, partner).wait_recv()
        kv_across(me - 2 * s).start()
        kv_share(me - 2 * s).start()
        return 0

    def pass_across(s, _):
        kv_across(partner - 2 * s).wait_recv()
        kv_share(partner - 2 * s).start()
        return 0

    def conv_flags(b, before):
        now = segs_of(b + 1)
        both_blocks = jnp.concatenate([before, now], axis=1)
        row = iota((8, tokens), 0)
        flags = now
        for back in range(1, taps):
            kept = (pltpu.roll(both_blocks, back, 1)[:, tokens:] == now).astype(F32)
            flags = jnp.where(row == back, kept, flags)
        eye = (iota((8, 8), 0) == iota((8, 8), 1)).astype(BF16)
        return dot(flags.astype(BF16), eye, (0, 0))

    def keeps_of(flags, n):
        return [jnp.broadcast_to(flags[:n, back : back + 1], (n, LANES)) > 0.5 for back in range(taps - 1, 0, -1)]

    def conv(pad, b, cols, keeps, weight_ref, n):
        acc = weight_ref[taps - 1 : taps, cols] * pad[b, RIM : RIM + n, cols]
        for k in range(taps - 1):
            first = RIM - (taps - 1) + k
            term = weight_ref[k : k + 1, cols] * pad[b, first : first + n, cols]
            acc = acc + jnp.where(keeps[k], term, 0.0)
        return jax.nn.silu(acc).astype(BF16)

    def conv_groups(b, kind, keeps, n):
        out = (conv_b, conv_c)[kind]
        for c in range(0, STATE_SIZE, LANES):
            at = slice(kind * STATE_SIZE + c, kind * STATE_SIZE + c + LANES)
            out[b, 0:n, c : c + LANES] = conv(pad_g, b, at, keeps, taps_groups_ref, n)

    def conv_inner(b, c, keeps, n):
        at = slice(c * LANES, (c + 1) * LANES)
        conv_x[b, 0:n, at] = conv(pad_x, b, at, keeps, taps_inner_ref, n)

    def rim_arrived(slot):
        for c in rim_copies(0, partner, slot, slot):
            c.wait_recv()

    def segs_of(at):
        return jnp.broadcast_to(segs_ref[at].astype(F32), (8, tokens))

    for w in (loads[0], *loads[3:7]):
        w.wait()
    pad_g[side, 0:RIM, :] = jnp.zeros((RIM, wide), F32)
    pad_x[side, 0:RIM, :] = jnp.zeros((RIM, half), F32)
    pad_g[side, RIM:, :] = g_in[side].astype(F32)
    pad_x[side, RIM:, :] = x_in[side].astype(F32)
    own_flags = conv_flags(side, jnp.full((8, tokens), -1.0, F32))
    own_keeps = keeps_of(own_flags, tokens)
    conv_groups(side, 0, own_keeps, tokens)
    conv_groups(side, 1, own_keeps, tokens)

    own_segs = jnp.broadcast_to(segs_ref[1 + side].astype(F32), (RIM, tokens)).astype(BF16)
    kv[me, 0, pl.ds(tokens, RIM), :] = own_segs
    kv[me, 1, pl.ds(tokens, RIM), :] = own_segs
    loads[1].wait()
    loads[2].wait()

    @pl.when(side == 0)
    def _():
        kv_across(me).start()

    @pl.when(has_upper)
    def _():
        pl.semaphore_wait(ready.at[upper], 1)

    @pl.when(has_upper & (side == 1))
    def _():
        pl.semaphore_wait(ready.at[following], 1)
        seg_copy(1, following, 0).start()
        seg_copy(2, upper, 0).start()
        for c in rim_skip():
            c.start()
        for c in rim_next():
            c.start()

    @pl.when(has_upper)
    def _():
        kv_copy(me, upper).start()

    for c in range(chunks):
        conv_inner(side, c, own_keeps, tokens)

    for w in loads[7:10]:
        w.wait()
    step_copy(other).wait_recv()
    seg_copy(0, partner, 1 + other).wait_recv()
    bias = column(bias_ref[...].reshape(1, heads))
    rates = jnp.exp(column(decay_ref[...].reshape(1, heads)))
    on_left = side == 0

    def mine_of(a):
        kept = jnp.where(on_left, a[:few], a[few:])
        return jnp.concatenate([kept, jnp.zeros((8 - few, a.shape[1]), F32)], axis=0)

    raw = mine_of(jnp.concatenate([step_in[0], step_in[1]], axis=1) + bias)
    steps = jnp.maximum(raw, 0.0) + jnp.log1p(jnp.exp(-jnp.abs(raw)))
    span = 2 * tokens
    row_t, col_t = iota((span, span), 0), iota((span, span), 1)
    upto = (row_t <= col_t).astype(BF16)
    sums = dot(thirds(-steps * mine_of(rates)), upto, (1, 0))
    cumul = sums[0:8] + sums[8:16] + sums[16:24]
    total = cumul[:, span - 1 : span]
    segs_rows8 = jnp.concatenate([segs_of(1), segs_of(2)], axis=1)
    last_seg = segs_rows8[:, span - 1 : span]
    weigh = jnp.where(segs_rows8 == last_seg, jnp.exp(total - cumul), 0.0) * steps
    cols = to_columns(jnp.concatenate([cumul, weigh, jnp.exp(cumul), segs_rows8], axis=0))
    left = iota((span, LANES), 1) < HEAD_CHANNELS

    def two_heads(base, c):
        a, b = base + 2 * c, base + 2 * c + 1
        return jnp.where(left, cols[:, a : a + 1], cols[:, b : b + 1])

    group_copy(other, 0).wait_recv()
    group_share(0).start()

    def send_far(s, _):
        pl.semaphore_wait(ready.at[me + 2 * s], 1)
        kv_copy(me, me + 2 * s).start()
        return 0

    lax.fori_loop(2, last_pair - pair + 1, send_far, 0)

    other_keeps = keeps_of(conv_flags(other, jnp.full((8, tokens), -1.0, F32)), tokens)
    pad_g[other, 0:RIM, :] = jnp.zeros((RIM, wide), F32)
    pad_x[other, 0:RIM, :] = jnp.zeros((RIM, half), F32)
    group_share(0).wait_recv()
    pad_g[other, RIM:, 0:STATE_SIZE] = g_in[other, :, 0:STATE_SIZE].astype(F32)
    conv_groups(other, 0, other_keeps, tokens)

    def conv_other(c):
        lanes = slice(c * LANES, (c + 1) * LANES)
        x_copy(other, c).wait_recv()
        pad_x[other, RIM:, lanes] = x_in[other, :, lanes].astype(F32)
        conv_inner(other, c, other_keeps, tokens)

    conv_other(0)

    @pl.when(has_lower)
    def _():
        seg_copy(0, partner, 0).wait_recv()
        rim_arrived(0)

    @pl.when(pair == 0)
    def _():
        segs_ref[0] = jnp.full((1, tokens), -1, jnp.int32)
        rim_x[0] = jnp.zeros_like(rim_x[0])
        rim_g[0] = jnp.zeros_like(rim_g[0])

    @pl.when(side == 1)
    def _():
        rim_arrived(1)

    @pl.when(side == 0)
    def _():
        rim_x[1] = x_in[0, tokens - RIM :, :]
        rim_g[1] = g_in[0, tokens - RIM :, :]

    first_keeps = []
    for b in range(2):
        pad_g[b, 0:RIM, :] = rim_g[b].astype(F32)
        pad_x[b, 0:RIM, :] = rim_x[b].astype(F32)
        first_keeps.append(keeps_of(conv_flags(b, segs_of(b)), RIM))
        conv_groups(b, 0, first_keeps[b], RIM)

    read_b = conv_b[...].reshape(span, STATE_SIZE)
    across_b = read_b.T

    def hop(src, dst, ss, rs, c, target):
        return remote(src.at[c], dst.at[c], ss.at[c], rs.at[c], at_seq(target))

    def e_hop(i, target):
        return hop(e_send, e_recv, e_ss, e_rs, i, target)

    for c in range(chunks):
        if c > 0:
            conv_other(c)
        for b in range(2):
            conv_inner(b, c, first_keeps[b], RIM)
        lanes = slice(c * LANES, (c + 1) * LANES)
        x = conv_x[:, :, lanes].reshape(span, LANES).astype(F32)
        state[:, lanes] = dot(across_b, (two_heads(8, c) * x).astype(BF16), (1, 0))

        @pl.when(pair == 0)
        def _():
            for r in range(PIECES):
                i = PIECES * c + r
                e_send[i] = state[r * depth : (r + 1) * depth, lanes].astype(BF16)
                e_hop(i, upper).start()

    group_copy(other, 1).wait_recv()
    group_share(1).start()

    prev_last = segs_of(0)[:, tokens - 1 : tokens]
    spread = iota((8, half), 1) // HEAD_CHANNELS == iota((8, half), 0)
    crossing_pair = jnp.where(last_seg == prev_last, jnp.exp(total), 0.0)
    through = jnp.sum(jnp.where(spread, crossing_pair, 0.0), axis=0, keepdims=True)
    joined = cols[:, 24:25] == prev_last[0:1]
    group_share(1).wait_recv()
    pad_g[other, RIM:, STATE_SIZE:] = g_in[other, :, STATE_SIZE:].astype(F32)
    conv_groups(other, 1, other_keeps, tokens)
    for b in range(2):
        conv_groups(b, 1, first_keeps[b], RIM)
    read_c = conv_c[...].reshape(span, STATE_SIZE)

    for w in weights:
        w.start()

    lax.fori_loop(1, pair + 1, pass_on, 0)

    for w in loads[10:]:
        w.wait()
    scale = 1.0 / math.sqrt(HD)
    queries = jnp.concatenate([query_ref[:, h * HD : (h + 1) * HD] for h in range(heads_here)], axis=0)
    rows = heads_here * tokens
    segs_q = jnp.concatenate([own_flags[:, 0:1]] * heads_here, axis=0)
    token_q = jnp.concatenate([iota((tokens, 1), 0)] * heads_here, axis=0)
    top_ref[...] = jnp.full((rows, 1), -1e30, F32)
    total_ref[...] = jnp.zeros((rows, 1), F32)
    summed_ref[...] = jnp.zeros((rows, HD), F32)

    def attend(k):
        @pl.when(k != me)
        def _():
            kv_share(k).wait_recv()

        scores = dot(queries, kv[k, 0, 0:tokens, :], (1, 1)) * scale
        segs_k = kv[k, 0, tokens:, :].astype(F32)[0:1, :tokens]
        allowed = (segs_k == segs_q) & (iota((rows, tokens), 1) + (k - me) * tokens <= token_q)
        scores = jnp.where(allowed, scores, -jnp.inf)
        top = top_ref[...]
        new_top = jnp.maximum(top, jnp.max(scores, axis=1, keepdims=True))
        rescale = jnp.exp(top - new_top)
        w = jnp.exp(scores - new_top)
        top_ref[...] = new_top
        total_ref[...] = total_ref[...] * rescale + jnp.sum(w, axis=1, keepdims=True)
        summed_ref[...] = summed_ref[...] * rescale + dot(w.astype(BF16), kv[k, 1, 0:tokens, :], (1, 0))

    same_head = (iota((2 * LANES, LANES), 0) % LANES // HEAD_CHANNELS == iota((2 * LANES, LANES), 1) // HEAD_CHANNELS).astype(
        BF16
    )
    gain_row = gain_ref[...].reshape(1, channels)
    gains = [
        jnp.where(on_left, gain_row[:, :half], gain_row[:, half:]),
        jnp.where(on_left, gain_row[:, half:], gain_row[:, :half]),
    ]

    def norm(which, c, gain, y):
        at = part(which, c)
        gated = y * jax.nn.silu(gate_ref[:, at].astype(F32))
        square = gated * gated
        high = square.astype(BF16)
        parts = jnp.concatenate([high, (square - high.astype(F32)).astype(BF16)], axis=1)
        mean_square = dot(parts, same_head, (1, 0)) * (1.0 / HEAD_CHANNELS)
        normed = gated * lax.rsqrt(mean_square + 1e-05) * gain[:, c * LANES : (c + 1) * LANES]
        both[:, at] = normed.astype(BF16)

    def f_hop(c):
        return hop(f_send, f_recv, f_ss, f_rs, c, partner)

    @pl.when(pair == 0)
    def _():
        e_recv[...] = jnp.zeros_like(e_recv)

    live = (cols[:, 24:25] == segs_rows8[0:1]) & (row_t >= col_t)
    crossing = dot(read_c, across_b, (1, 0))
    for c in range(chunks):
        lanes = slice(c * LANES, (c + 1) * LANES)
        x = conv_x[:, :, lanes].reshape(span, LANES)
        got = []
        for h in (2 * c, 2 * c + 1):
            halves = []
            for rows_of, width in ((slice(0, tokens), tokens), (slice(tokens, span), span)):
                gap = cols[rows_of, h : h + 1] - cumul[h : h + 1, :width]
                decays = jnp.exp(jnp.where(live[rows_of, :width], gap, -jnp.inf))
                mixing = (crossing[rows_of, :width] * decays * steps[h : h + 1, :width]).astype(BF16)
                halves.append(dot(mixing, x[:width], (1, 0)))
            got.append(jnp.concatenate(halves, axis=0))
        y_ref[:, lanes] = jnp.where(left, got[0], got[1])

    def attention():
        lax.fori_loop(0, pair + 1, lambda s, _: attend(me - 2 * s) or 0, 0)
        lax.fori_loop(other, pair + 1, pass_across, 0)
        lax.fori_loop(other, pair + 1, lambda s, _: attend(partner - 2 * s) or 0, 0)
        attended = (summed_ref[...] / total_ref[...]).astype(BF16)
        for h in range(heads_here):
            both[:, channels + h * HD : channels + (h + 1) * HD] = attended[h * tokens : (h + 1) * tokens]

    pl.when(pair == last_pair)(attention)
    for c in range(chunks):
        lanes = slice(c * LANES, (c + 1) * LANES)

        @pl.when(has_lower)
        def _():
            for r in range(PIECES):
                i = PIECES * c + r
                e_hop(i, partner).wait_recv()

                @pl.when(has_upper)
                def _():
                    enters = e_recv[i].astype(F32)
                    e_send[i] = (through[:, lanes] * enters + state[r * depth : (r + 1) * depth, lanes]).astype(BF16)
                    e_hop(i, upper).start()

        enters = jnp.concatenate([e_recv[PIECES * c + r] for r in range(PIECES)], axis=0)
        carried = jnp.where(joined, two_heads(16, c), 0.0) * dot(read_c, enters, (1, 0))
        y = y_ref[:, lanes] + carried
        f_send[c] = jnp.where(on_left, y[tokens:], y[:tokens]).astype(BF16)
        f_hop(c).start()
        norm(side, c, gains[0], jnp.where(on_left, y[:tokens], y[tokens:]))

    pl.when(pair < last_pair)(attention)
    for c in range(chunks):
        f_hop(c).wait_recv()
        norm(other, c, gains[1], f_recv[c].astype(F32))

    for w in weights:
        w.wait()
    width = out_ref.shape[1]

    def product(j, part_of):
        at = pl.ds(pl.multiple_of(j * width + part_of * (width // 2), LANES), width // 2)
        return dot(both[:, :channels], mproj[:, at], (1, 0)) + dot(both[:, channels:], aproj[:, at], (1, 0))

    def rs_copy(i, target):
        return remote(rs_send.at[i], rs_recv.at[i], rs_ss.at[i], rs_rs.at[i], at_head(target))

    to_pair = [rs_copy(h, sibling) for h in range(2)]
    to_sibling = [rs_copy(2 + h, sibling) for h in range(2)]
    to_opposite = [rs_copy(4 + h, opposite) for h in range(2)]
    for h in range(2):
        rs_send[h] = product(opposite_sibling, h).astype(BF16)
        to_pair[h].start()
    for h in range(2):
        away = product(opposite, h)
        to_pair[h].wait_recv()
        rs_send[4 + h] = (away + rs_recv[h].astype(F32)).astype(BF16)
        to_opposite[h].start()
    for h in range(2):
        rs_send[2 + h] = product(sibling, h).astype(BF16)
        to_sibling[h].start()
    for h in range(2):
        result = product(mine, h)
        to_sibling[h].wait_recv()
        result = result + rs_recv[2 + h].astype(F32)
        to_opposite[h].wait_recv()
        out_ref[:, h * (width // 2) : (h + 1) * (width // 2)] = (result + rs_recv[4 + h].astype(F32)).astype(BF16)

    for copy in (*to_pair, *to_sibling, *to_opposite, step_copy(side)):
        copy.wait_send()
    for c in range(chunks):
        x_copy(side, c).wait_send()
        f_hop(c).wait_send()
    for kind in range(2):
        group_copy(side, kind).wait_send()
        group_share(kind).wait_send()
    seg_copy(0, partner, 1 + side).wait_send()

    @pl.when(me < n_seq - 1)
    def _():
        for c in rim_next():
            c.wait_send()

    @pl.when(has_upper & (side == 1))
    def _():
        for c in rim_skip():
            c.wait_send()
        seg_copy(1, following, 0).wait_send()
        seg_copy(2, upper, 0).wait_send()

    @pl.when(has_upper)
    def _():
        for i in range(PIECES * chunks):
            e_hop(i, upper).wait_send()

    def sent_kv(s, _):
        kv_copy(me, me + 2 * s).wait_send()
        return 0

    lax.fori_loop(1, last_pair - pair + 1, sent_kv, 0)

    def sent_on(s, _):
        kv_across(me - 2 * s).wait_send()
        kv_share(me - 2 * s).wait_send()
        return 0

    lax.fori_loop(1, pair + 1, sent_on, 0)

    @pl.when(side == 0)
    def _():
        kv_across(me).wait_send()

    def sent_share(s, _):
        kv_share(partner - 2 * s).wait_send()
        return 0

    lax.fori_loop(other, pair + 1, sent_share, 0)


def shards(n_seq, n_head, *arrays):
    (inner, groups, gate, step, bias, decay, taps_i, taps_g, gain, query, key, value, segs, mproj, aproj) = arrays
    tokens, channels = inner.shape
    half = channels // 2
    wide = groups.shape[1]
    out_width = mproj.shape[1] // n_head
    chunks = half // LANES
    vmem = pl.BlockSpec(memory_space=pltpu.VMEM)
    hbm = pl.BlockSpec(memory_space=pltpu.HBM)
    dma = pltpu.SemaphoreType.DMA
    scratch = [
        pltpu.VMEM((3, 1, tokens), segs.dtype),
        pltpu.VMEM((2, *step.shape), F32),
        pltpu.VMEM(bias.shape, F32),
        pltpu.VMEM(decay.shape, F32),
        pltpu.VMEM((taps_i.shape[0], half), F32),
        pltpu.VMEM(taps_g.shape, F32),
        pltpu.VMEM(gain.shape, F32),
        pltpu.VMEM(query.shape, BF16),
        pltpu.VMEM(gate.shape, BF16),
        pltpu.VMEM((2, tokens, half), BF16),
        pltpu.VMEM((2, tokens, wide), BF16),
        pltpu.VMEM((2, RIM, half), BF16),
        pltpu.VMEM((2, RIM, wide), BF16),
        pltpu.VMEM((n_seq, 2, tokens + RIM, HD), BF16),
        pltpu.VMEM((2, RIM + tokens, half), F32),
        pltpu.VMEM((2, RIM + tokens, wide), F32),
        pltpu.VMEM((2, tokens, half), BF16),
        pltpu.VMEM((2, tokens, STATE_SIZE), BF16),
        pltpu.VMEM((2, tokens, STATE_SIZE), BF16),
        pltpu.VMEM((2 * tokens, half), F32),
        pltpu.VMEM((STATE_SIZE, half), F32),
        *[pltpu.VMEM((PIECES * chunks, STATE_SIZE // PIECES, LANES), BF16) for _ in range(2)],
        *[pltpu.VMEM((chunks, tokens, LANES), BF16) for _ in range(2)],
        pltpu.VMEM((tokens, channels + query.shape[1]), BF16),
        pltpu.VMEM(mproj.shape, BF16),
        pltpu.VMEM(aproj.shape, BF16),
        pltpu.VMEM((6, tokens, out_width // 2), BF16),
        pltpu.VMEM((6, tokens, out_width // 2), BF16),
        *[pltpu.VMEM((query.shape[1] // HD * tokens, n), F32) for n in (1, 1, HD)],
        pltpu.SemaphoreType.REGULAR((n_seq,)),
        dma((13,)),
        dma((2,)),
        dma((chunks,)),
        dma((chunks,)),
        dma((4,)),
        dma((4,)),
        dma((2,)),
        dma((2, 2)),
        dma((2, 2)),
        dma((3,)),
        dma((3,)),
        *[dma((n_seq,)) for _ in range(5)],
        *[dma((PIECES * chunks,)) for _ in range(2)],
        *[dma((chunks,)) for _ in range(2)],
        dma((6,)),
        dma((6,)),
    ]
    return pl.pallas_call(
        functools.partial(kernel, n_seq, n_head),
        out_shape=jax.ShapeDtypeStruct((tokens, out_width), BF16),
        in_specs=[hbm] * 15,
        out_specs=vmem,
        scratch_shapes=scratch,
        compiler_params=pltpu.CompilerParams(
            collective_id=0, has_side_effects=True, vmem_limit_bytes=64 * 2**20
        ),
        name="mixer",
    )(*arrays)


def solution(mesh):
    placed = (
        P("seq", "head"),
        P("seq", None),
        P("seq", "head"),
        P("head", "seq"),
        P("head"),
        P("head"),
        P(None, "head"),
        P(),
        P("head"),
        P("seq", "head"),
        P("seq", None),
        P("seq", None),
        P("seq"),
        P("head", None),
        P("head", None),
    )
    return jax.shard_map(
        functools.partial(shards, mesh.shape["seq"], mesh.shape["head"]),
        mesh=mesh,
        in_specs=placed,
        out_specs=P("seq", "head"),
        check_vma=False,
    )
```

```python
import functools
import math

import jax
import jax.numpy as jnp
from jax import lax
from jax.experimental import pallas as pl
from jax.experimental.pallas import tpu as pltpu
from jax.sharding import PartitionSpec as P

HEAD_CHANNELS = 64
STATE_SIZE = 256
QH = 8
KVH = 2
HD = 128
LANES = 128
RIM = 16
PIECES = 4
F32 = jnp.float32
BF16 = jnp.bfloat16
MESH = pl.DeviceIdType.MESH


def dot(a, b, contract):
    return lax.dot_general(a, b, ((contract[:1], contract[1:]), ((), ())), preferred_element_type=F32)


def iota(shape, axis):
    return lax.broadcasted_iota(jnp.int32, shape, axis)


def column(row):
    n = row.shape[1]
    eye = iota((n, n), 0) == iota((n, n), 1)
    return jnp.sum(jnp.where(eye, jnp.broadcast_to(row, (n, n)), 0.0), axis=1, keepdims=True)


def thirds(a):
    high = a.astype(BF16).astype(F32)
    rest = a - high
    middle = rest.astype(BF16).astype(F32)
    return jnp.concatenate([high, middle, rest - middle], axis=0).astype(BF16)


def to_columns(rows):
    n = rows.shape[0]
    pick = (iota((3 * n, n), 0) % n == iota((3 * n, n), 1)).astype(BF16)
    return dot(thirds(rows), pick, (0, 0))


def kernel(
    n_seq,
    n_head,
    inner_hbm,
    groups_hbm,
    gate_hbm,
    step_hbm,
    bias_hbm,
    decay_hbm,
    taps_inner_hbm,
    taps_groups_hbm,
    gain_hbm,
    query_hbm,
    key_hbm,
    value_hbm,
    segs_hbm,
    mamba_proj_hbm,
    attn_proj_hbm,
    out_ref,
    segs_ref,
    step_in,
    bias_ref,
    decay_ref,
    taps_inner_ref,
    taps_groups_ref,
    gain_ref,
    query_ref,
    gate_ref,
    x_in,
    g_in,
    rim_x,
    rim_g,
    kv,
    pad_x,
    pad_g,
    conv_x,
    conv_b,
    conv_c,
    y_ref,
    state,
    e_send,
    e_recv,
    f_send,
    f_recv,
    both,
    mproj,
    aproj,
    rs_send,
    rs_recv,
    scores_ref,
    top_ref,
    total_ref,
    summed_ref,
    ready,
    load_sem,
    weight_sem,
    x_ss,
    x_rs,
    g_ss,
    g_rs,
    step_sem,
    rim_ss,
    rim_rs,
    seg_ss,
    seg_rs,
    kv_ss,
    across_ss,
    kv_rs,
    share_ss,
    share_rs,
    e_ss,
    e_rs,
    f_ss,
    f_rs,
    rs_ss,
    rs_rs,
):
    tokens, channels = gate_ref.shape
    heads = step_in.shape[1]
    half = channels // 2
    few = heads // 2
    chunks = half // LANES
    wide = groups_hbm.shape[1]
    taps = taps_inner_ref.shape[0]
    depth = STATE_SIZE // PIECES
    heads_here = query_ref.shape[1] // HD
    me = lax.axis_index("seq")
    mine = lax.axis_index("head")
    pair, side = me // 2, me % 2
    other = 1 - side
    last_pair = n_seq // 2 - 1
    partner = me + 1 - 2 * side
    upper = lax.min(me + 2, n_seq - 1)
    lower = lax.max(me - 2, 0)
    following = lax.min(me + 1, n_seq - 1)
    previous = lax.max(me - 1, 0)
    core = mine % 2
    sibling = mine + 1 - 2 * core
    opposite = (mine + 2) % n_head
    opposite_sibling = (sibling + 2) % n_head
    has_upper, has_lower = pair < last_pair, pair > 0

    def at_seq(s):
        return (s, mine)

    def at_head(h):
        return (me, h)

    def remote(src, dst, ss, rs, target):
        return pltpu.make_async_remote_copy(src, dst, ss, rs, device_id=target, device_id_type=MESH)

    def part(which, c):
        return pl.ds(pl.multiple_of(which * half + c * LANES, LANES), LANES)

    def side_half(which):
        return pl.ds(pl.multiple_of(which * half, LANES), half)

    def core_cols(kind):
        return pl.ds(pl.multiple_of(kind * STATE_SIZE + core * LANES, LANES), LANES)

    kv_head = mine * heads_here // (QH // KVH)
    kv_cols = pl.ds(pl.multiple_of(kv_head * HD, HD), HD)
    body = pl.ds(0, tokens)

    weights = [
        pltpu.make_async_copy(mamba_proj_hbm, mproj, weight_sem.at[0]),
        pltpu.make_async_copy(attn_proj_hbm, aproj, weight_sem.at[1]),
    ]
    loads = [
        pltpu.make_async_copy(src, dst, load_sem.at[i])
        for i, (src, dst) in enumerate(
            (
                (segs_hbm, segs_ref.at[1 + side, 0]),
                (key_hbm.at[:, kv_cols], kv.at[me, 0, body]),
                (value_hbm.at[:, kv_cols], kv.at[me, 1, body]),
                (groups_hbm, g_in.at[side]),
                (taps_groups_hbm, taps_groups_ref),
                (inner_hbm.at[:, side_half(side)], x_in.at[side]),
                (taps_inner_hbm.at[:, side_half(side)], taps_inner_ref),
                (step_hbm, step_in.at[side]),
                (bias_hbm, bias_ref),
                (decay_hbm, decay_ref),
                (query_hbm, query_ref),
                (gate_hbm, gate_ref),
                (gain_hbm, gain_ref),
            )
        )
    ]

    barrier = pltpu.get_barrier_semaphore()

    def hello(target):
        pl.semaphore_signal(barrier, inc=1, device_id=target, device_id_type=MESH)

    hello(at_seq(partner))
    hello(at_head(sibling))
    hello(at_head(opposite))

    def hello_later(s, _):
        hello(at_seq(me + 2 * s))
        return 0

    lax.fori_loop(1, last_pair - pair + 1, hello_later, 0)

    @pl.when(has_upper & (side == 1))
    def _():
        hello(at_seq(following))

    for w in loads:
        w.start()
    pl.semaphore_wait(barrier, 3 + pair + jnp.where(has_lower, other, 0))

    def answer(k):
        pl.semaphore_signal(ready.at[me], inc=1, device_id=at_seq(k), device_id_type=MESH)

    @pl.when(has_lower & (side == 0))
    def _():
        answer(previous)

    lax.fori_loop(1, pair + 1, lambda s, _: answer(me - 2 * s) or 0, 0)

    tail_rows = pl.ds(tokens - RIM, RIM)

    def rim_copies(kind, target, slot, which):
        return [
            remote(
                inner_hbm.at[tail_rows, side_half(which)], rim_x.at[slot], rim_ss.at[kind, 0], rim_rs.at[slot, 0], at_seq(target)
            ),
            remote(groups_hbm.at[tail_rows, :], rim_g.at[slot], rim_ss.at[kind, 1], rim_rs.at[slot, 1], at_seq(target)),
        ]

    def rim_next():
        return rim_copies(0, following, other, other)

    def rim_skip():
        return rim_copies(1, upper, 0, side)

    def group_copy(block, kind):
        at = core_cols(kind)
        return remote(groups_hbm.at[:, at], g_in.at[block, :, at], g_ss.at[kind], g_rs.at[kind], at_seq(partner))

    def group_share(kind):
        at = core_cols(kind)
        return remote(g_in.at[other, :, at], g_in.at[other, :, at], g_ss.at[2 + kind], g_rs.at[2 + kind], at_head(sibling))

    def x_copy(block, c):
        return remote(
            inner_hbm.at[:, part(other, c)],
            x_in.at[block, :, pl.ds(c * LANES, LANES)],
            x_ss.at[c],
            x_rs.at[c],
            at_seq(partner),
        )

    def step_copy(block):
        return remote(step_hbm, step_in.at[block], step_sem.at[0], step_sem.at[1], at_seq(partner))

    def seg_copy(kind, target, dst):
        return remote(segs_hbm, segs_ref.at[dst, 0], seg_ss.at[kind], seg_rs.at[dst], at_seq(target))

    step_copy(side).start()
    seg_copy(0, partner, 1 + side).start()

    group_copy(side, 0).start()
    x_copy(side, 0).start()

    @pl.when(side == 0)
    def _():
        for c in rim_next():
            c.start()

    for c in range(1, chunks):
        x_copy(side, c).start()
    group_copy(side, 1).start()

    def kv_copy(b, k):
        return remote(kv.at[b, core], kv.at[b, core], kv_ss.at[k], kv_rs.at[b], at_seq(k))

    def kv_share(b):
        return remote(kv.at[b, core], kv.at[b, core], share_ss.at[b], share_rs.at[b], at_head(sibling))

    def kv_across(b):
        return remote(kv.at[b, core], kv.at[b, core], across_ss.at[b], kv_rs.at[b], at_seq(partner))

    def pass_on(s, _):
        kv_copy(me - 2 * s, partner).wait_recv()
        kv_across(me - 2 * s).start()
        kv_share(me - 2 * s).start()
        return 0

    def pass_across(s, _):
        kv_across(partner - 2 * s).wait_recv()
        kv_share(partner - 2 * s).start()
        return 0

    def conv_flags(b, before):
        now = segs_of(b + 1)
        both_blocks = jnp.concatenate([before, now], axis=1)
        row = iota((8, tokens), 0)
        flags = now
        for back in range(1, taps):
            kept = (pltpu.roll(both_blocks, back, 1)[:, tokens:] == now).astype(F32)
            flags = jnp.where(row == back, kept, flags)
        eye = (iota((8, 8), 0) == iota((8, 8), 1)).astype(BF16)
        return dot(flags.astype(BF16), eye, (0, 0))

    def keeps_of(flags, n):
        return [jnp.broadcast_to(flags[:n, back : back + 1], (n, LANES)) > 0.5 for back in range(taps - 1, 0, -1)]

    def conv(pad, b, cols, keeps, weight_ref, n):
        acc = weight_ref[taps - 1 : taps, cols] * pad[b, RIM : RIM + n, cols]
        for k in range(taps - 1):
            first = RIM - (taps - 1) + k
            term = weight_ref[k : k + 1, cols] * pad[b, first : first + n, cols]
            acc = acc + jnp.where(keeps[k], term, 0.0)
        return jax.nn.silu(acc).astype(BF16)

    def conv_groups(b, kind, keeps, n):
        out = (conv_b, conv_c)[kind]
        for c in range(0, STATE_SIZE, LANES):
            at = slice(kind * STATE_SIZE + c, kind * STATE_SIZE + c + LANES)
            out[b, 0:n, c : c + LANES] = conv(pad_g, b, at, keeps, taps_groups_ref, n)

    def conv_inner(b, c, keeps, n):
        at = slice(c * LANES, (c + 1) * LANES)
        conv_x[b, 0:n, at] = conv(pad_x, b, at, keeps, taps_inner_ref, n)

    def rim_arrived(slot):
        for c in rim_copies(0, partner, slot, slot):
            c.wait_recv()

    def segs_of(at):
        return jnp.broadcast_to(segs_ref[at].astype(F32), (8, tokens))

    for w in (loads[0], *loads[3:7]):
        w.wait()
    pad_g[side, 0:RIM, :] = jnp.zeros((RIM, wide), F32)
    pad_x[side, 0:RIM, :] = jnp.zeros((RIM, half), F32)
    pad_g[side, RIM:, :] = g_in[side].astype(F32)
    pad_x[side, RIM:, :] = x_in[side].astype(F32)
    own_flags = conv_flags(side, jnp.full((8, tokens), -1.0, F32))
    own_keeps = keeps_of(own_flags, tokens)
    conv_groups(side, 0, own_keeps, tokens)

    own_segs = jnp.broadcast_to(segs_ref[1 + side].astype(F32), (RIM, tokens)).astype(BF16)
    kv[me, 0, pl.ds(tokens, RIM), :] = own_segs
    kv[me, 1, pl.ds(tokens, RIM), :] = own_segs
    loads[1].wait()
    loads[2].wait()

    @pl.when(side == 0)
    def _():
        kv_across(me).start()

    @pl.when(has_upper)
    def _():
        pl.semaphore_wait(ready.at[upper], 1)

    @pl.when(has_upper & (side == 1))
    def _():
        pl.semaphore_wait(ready.at[following], 1)
        seg_copy(1, following, 0).start()
        seg_copy(2, upper, 0).start()
        for c in rim_skip():
            c.start()
        for c in rim_next():
            c.start()

    @pl.when(has_upper)
    def _():
        kv_copy(me, upper).start()

    for c in range(chunks):
        conv_inner(side, c, own_keeps, tokens)

    for w in loads[7:10]:
        w.wait()
    step_copy(other).wait_recv()
    seg_copy(0, partner, 1 + other).wait_recv()
    bias = column(bias_ref[...].reshape(1, heads))
    rates = jnp.exp(column(decay_ref[...].reshape(1, heads)))
    on_left = side == 0

    def mine_of(a):
        kept = jnp.where(on_left, a[:few], a[few:])
        return jnp.concatenate([kept, jnp.zeros((8 - few, a.shape[1]), F32)], axis=0)

    raw = mine_of(jnp.concatenate([step_in[0], step_in[1]], axis=1) + bias)
    steps = jnp.maximum(raw, 0.0) + jnp.log1p(jnp.exp(-jnp.abs(raw)))
    span = 2 * tokens
    row_t, col_t = iota((span, span), 0), iota((span, span), 1)
    upto = (row_t <= col_t).astype(BF16)
    sums = dot(thirds(-steps * mine_of(rates)), upto, (1, 0))
    cumul = sums[0:8] + sums[8:16] + sums[16:24]
    total = cumul[:, span - 1 : span]
    segs_rows8 = jnp.concatenate([segs_of(1), segs_of(2)], axis=1)
    last_seg = segs_rows8[:, span - 1 : span]
    weigh = jnp.where(segs_rows8 == last_seg, jnp.exp(total - cumul), 0.0) * steps
    cols = to_columns(jnp.concatenate([cumul, weigh, jnp.exp(cumul), segs_rows8], axis=0))
    left = iota((span, LANES), 1) < HEAD_CHANNELS

    def two_heads(base, c):
        a, b = base + 2 * c, base + 2 * c + 1
        return jnp.where(left, cols[:, a : a + 1], cols[:, b : b + 1])

    group_copy(other, 0).wait_recv()
    group_share(0).start()

    def send_far(s, _):
        pl.semaphore_wait(ready.at[me + 2 * s], 1)
        kv_copy(me, me + 2 * s).start()
        return 0

    lax.fori_loop(2, last_pair - pair + 1, send_far, 0)

    other_keeps = keeps_of(conv_flags(other, jnp.full((8, tokens), -1.0, F32)), tokens)
    pad_g[other, 0:RIM, :] = jnp.zeros((RIM, wide), F32)
    pad_x[other, 0:RIM, :] = jnp.zeros((RIM, half), F32)
    group_share(0).wait_recv()
    pad_g[other, RIM:, 0:STATE_SIZE] = g_in[other, :, 0:STATE_SIZE].astype(F32)
    conv_groups(other, 0, other_keeps, tokens)

    def conv_other(c):
        lanes = slice(c * LANES, (c + 1) * LANES)
        x_copy(other, c).wait_recv()
        pad_x[other, RIM:, lanes] = x_in[other, :, lanes].astype(F32)
        conv_inner(other, c, other_keeps, tokens)

    conv_other(0)

    @pl.when(has_lower)
    def _():
        seg_copy(0, partner, 0).wait_recv()
        rim_arrived(0)

    @pl.when(pair == 0)
    def _():
        segs_ref[0] = jnp.full((1, tokens), -1, jnp.int32)
        rim_x[0] = jnp.zeros_like(rim_x[0])
        rim_g[0] = jnp.zeros_like(rim_g[0])

    @pl.when(side == 1)
    def _():
        rim_arrived(1)

    @pl.when(side == 0)
    def _():
        rim_x[1] = x_in[0, tokens - RIM :, :]
        rim_g[1] = g_in[0, tokens - RIM :, :]

    first_keeps = []
    for b in range(2):
        pad_g[b, 0:RIM, :] = rim_g[b].astype(F32)
        pad_x[b, 0:RIM, :] = rim_x[b].astype(F32)
        first_keeps.append(keeps_of(conv_flags(b, segs_of(b)), RIM))
        conv_groups(b, 0, first_keeps[b], RIM)

    read_b = conv_b[...].reshape(span, STATE_SIZE)
    across_b = read_b.T

    def hop(src, dst, ss, rs, c, target):
        return remote(src.at[c], dst.at[c], ss.at[c], rs.at[c], at_seq(target))

    def e_hop(i, target):
        return hop(e_send, e_recv, e_ss, e_rs, i, target)

    for c in range(chunks):
        if c > 0:
            conv_other(c)
        for b in range(2):
            conv_inner(b, c, first_keeps[b], RIM)
        lanes = slice(c * LANES, (c + 1) * LANES)
        x = conv_x[:, :, lanes].reshape(span, LANES).astype(F32)
        state[:, lanes] = dot(across_b, (two_heads(8, c) * x).astype(BF16), (1, 0))

        @pl.when(pair == 0)
        def _():
            for r in range(PIECES):
                i = PIECES * c + r
                e_send[i] = state[r * depth : (r + 1) * depth, lanes].astype(BF16)
                e_hop(i, upper).start()

    group_copy(other, 1).wait_recv()
    group_share(1).start()
    pad_g[side, 0:RIM, STATE_SIZE:] = jnp.zeros((RIM, STATE_SIZE), F32)
    conv_groups(side, 1, own_keeps, tokens)
    pad_g[side, 0:RIM, STATE_SIZE:] = rim_g[side, :, STATE_SIZE:].astype(F32)

    prev_last = segs_of(0)[:, tokens - 1 : tokens]
    spread = iota((8, half), 1) // HEAD_CHANNELS == iota((8, half), 0)
    crossing_pair = jnp.where(last_seg == prev_last, jnp.exp(total), 0.0)
    through = jnp.sum(jnp.where(spread, crossing_pair, 0.0), axis=0, keepdims=True)
    joined = cols[:, 24:25] == prev_last[0:1]
    group_share(1).wait_recv()
    pad_g[other, RIM:, STATE_SIZE:] = g_in[other, :, STATE_SIZE:].astype(F32)
    conv_groups(other, 1, other_keeps, tokens)
    for b in range(2):
        conv_groups(b, 1, first_keeps[b], RIM)
    read_c = conv_c[...].reshape(span, STATE_SIZE)

    for w in weights:
        w.start()

    lax.fori_loop(1, pair + 1, pass_on, 0)

    for w in loads[10:]:
        w.wait()
    scale = 1.0 / math.sqrt(HD)
    queries = jnp.concatenate([query_ref[:, h * HD : (h + 1) * HD] for h in range(heads_here)], axis=0)
    rows = heads_here * tokens
    segs_q = jnp.concatenate([own_flags[:, 0:1]] * heads_here, axis=0)
    token_q = jnp.concatenate([iota((tokens, 1), 0)] * heads_here, axis=0)
    top_ref[...] = jnp.full((rows, tokens), -jnp.inf, F32)
    total_ref[...] = jnp.zeros((rows, tokens), F32)
    summed_ref[...] = jnp.zeros((rows, HD), F32)

    def attend(k):
        @pl.when(k != me)
        def _():
            kv_share(k).wait_recv()

        scores = dot(queries, kv[k, 0, 0:tokens, :], (1, 1)) * scale
        segs_k = kv[k, 0, tokens:, :].astype(F32)[0:1, :tokens]
        allowed = (segs_k == segs_q) & (iota((rows, tokens), 1) + (k - me) * tokens <= token_q)
        scores = jnp.where(allowed, scores, -jnp.inf)
        scores_ref[k] = scores
        top_ref[...] = jnp.maximum(top_ref[...], scores)

    same_head = (iota((2 * LANES, LANES), 0) % LANES // HEAD_CHANNELS == iota((2 * LANES, LANES), 1) // HEAD_CHANNELS).astype(
        BF16
    )
    gain_row = gain_ref[...].reshape(1, channels)
    gains = [
        jnp.where(on_left, gain_row[:, :half], gain_row[:, half:]),
        jnp.where(on_left, gain_row[:, half:], gain_row[:, :half]),
    ]

    def norm(which, c, gain, y):
        at = part(which, c)
        gated = y * jax.nn.silu(gate_ref[:, at].astype(F32))
        square = gated * gated
        high = square.astype(BF16)
        parts = jnp.concatenate([high, (square - high.astype(F32)).astype(BF16)], axis=1)
        mean_square = dot(parts, same_head, (1, 0)) * (1.0 / HEAD_CHANNELS)
        normed = gated * lax.rsqrt(mean_square + 1e-05) * gain[:, c * LANES : (c + 1) * LANES]
        both[:, at] = normed.astype(BF16)

    def f_hop(c):
        return hop(f_send, f_recv, f_ss, f_rs, c, partner)

    @pl.when(pair == 0)
    def _():
        e_recv[...] = jnp.zeros_like(e_recv)

    live = (cols[:, 24:25] == segs_rows8[0:1]) & (row_t >= col_t)
    crossing = dot(read_c, across_b, (1, 0))
    for c in range(chunks):
        lanes = slice(c * LANES, (c + 1) * LANES)
        x = conv_x[:, :, lanes].reshape(span, LANES)
        got = []
        for h in (2 * c, 2 * c + 1):
            halves = []
            for rows_of, width in ((slice(0, tokens), tokens), (slice(tokens, span), span)):
                gap = cols[rows_of, h : h + 1] - cumul[h : h + 1, :width]
                decays = jnp.exp(jnp.where(live[rows_of, :width], gap, -jnp.inf))
                mixing = (crossing[rows_of, :width] * decays * steps[h : h + 1, :width]).astype(BF16)
                halves.append(dot(mixing, x[:width], (1, 0)))
            got.append(jnp.concatenate(halves, axis=0))
        y_ref[:, lanes] = jnp.where(left, got[0], got[1])

    def attend_line():
        lax.fori_loop(0, pair + 1, lambda s, _: attend(me - 2 * s) or 0, 0)
        lax.fori_loop(other, pair + 1, pass_across, 0)

    def attend_rest():
        lax.fori_loop(other, pair + 1, lambda s, _: attend(partner - 2 * s) or 0, 0)
        top = jnp.max(top_ref[...], axis=1, keepdims=True)

        def add(k, _):
            w = jnp.exp(scores_ref[k] - top)
            total_ref[...] += w
            summed_ref[...] += dot(w.astype(BF16), kv[k, 1, 0:tokens, :], (1, 0))
            return 0

        lax.fori_loop(0, me + 1, add, 0)
        attended = (summed_ref[...] / jnp.sum(total_ref[...], axis=1, keepdims=True)).astype(BF16)
        for h in range(heads_here):
            both[:, channels + h * HD : channels + (h + 1) * HD] = attended[h * tokens : (h + 1) * tokens]

    pl.when(pair == last_pair)(attend_line)
    for c in range(chunks):
        lanes = slice(c * LANES, (c + 1) * LANES)

        @pl.when(has_lower)
        def _():
            for r in range(PIECES):
                i = PIECES * c + r
                e_hop(i, partner).wait_recv()

                @pl.when(has_upper)
                def _():
                    enters = e_recv[i].astype(F32)
                    e_send[i] = (through[:, lanes] * enters + state[r * depth : (r + 1) * depth, lanes]).astype(BF16)
                    e_hop(i, upper).start()

        enters = jnp.concatenate([e_recv[PIECES * c + r] for r in range(PIECES)], axis=0)
        carried = jnp.where(joined, two_heads(16, c), 0.0) * dot(read_c, enters, (1, 0))
        y = y_ref[:, lanes] + carried
        f_send[c] = jnp.where(on_left, y[tokens:], y[:tokens]).astype(BF16)
        f_hop(c).start()
        norm(side, c, gains[0], jnp.where(on_left, y[:tokens], y[tokens:]))

    pl.when(pair < last_pair)(attend_line)
    attend_rest()
    for c in range(chunks):
        f_hop(c).wait_recv()
        norm(other, c, gains[1], f_recv[c].astype(F32))

    for w in weights:
        w.wait()
    width = out_ref.shape[1]

    def product(j, part_of):
        at = pl.ds(pl.multiple_of(j * width + part_of * (width // 2), LANES), width // 2)
        return dot(both[:, :channels], mproj[:, at], (1, 0)) + dot(both[:, channels:], aproj[:, at], (1, 0))

    def rs_copy(i, target):
        return remote(rs_send.at[i], rs_recv.at[i], rs_ss.at[i], rs_rs.at[i], at_head(target))

    to_pair = [rs_copy(h, sibling) for h in range(2)]
    to_sibling = [rs_copy(2 + h, sibling) for h in range(2)]
    to_opposite = [rs_copy(4 + h, opposite) for h in range(2)]
    for h in range(2):
        rs_send[h] = product(opposite_sibling, h).astype(BF16)
        to_pair[h].start()
    for h in range(2):
        away = product(opposite, h)
        to_pair[h].wait_recv()
        rs_send[4 + h] = (away + rs_recv[h].astype(F32)).astype(BF16)
        to_opposite[h].start()
    for h in range(2):
        rs_send[2 + h] = product(sibling, h).astype(BF16)
        to_sibling[h].start()
    for h in range(2):
        result = product(mine, h)
        to_sibling[h].wait_recv()
        result = result + rs_recv[2 + h].astype(F32)
        to_opposite[h].wait_recv()
        out_ref[:, h * (width // 2) : (h + 1) * (width // 2)] = (result + rs_recv[4 + h].astype(F32)).astype(BF16)

    for copy in (*to_pair, *to_sibling, *to_opposite, step_copy(side)):
        copy.wait_send()
    for c in range(chunks):
        x_copy(side, c).wait_send()
        f_hop(c).wait_send()
    for kind in range(2):
        group_copy(side, kind).wait_send()
        group_share(kind).wait_send()
    seg_copy(0, partner, 1 + side).wait_send()

    @pl.when(me < n_seq - 1)
    def _():
        for c in rim_next():
            c.wait_send()

    @pl.when(has_upper & (side == 1))
    def _():
        for c in rim_skip():
            c.wait_send()
        seg_copy(1, following, 0).wait_send()
        seg_copy(2, upper, 0).wait_send()

    @pl.when(has_upper)
    def _():
        for i in range(PIECES * chunks):
            e_hop(i, upper).wait_send()

    def sent_kv(s, _):
        kv_copy(me, me + 2 * s).wait_send()
        return 0

    lax.fori_loop(1, last_pair - pair + 1, sent_kv, 0)

    def sent_on(s, _):
        kv_across(me - 2 * s).wait_send()
        kv_share(me - 2 * s).wait_send()
        return 0

    lax.fori_loop(1, pair + 1, sent_on, 0)

    @pl.when(side == 0)
    def _():
        kv_across(me).wait_send()

    def sent_share(s, _):
        kv_share(partner - 2 * s).wait_send()
        return 0

    lax.fori_loop(other, pair + 1, sent_share, 0)


def shards(n_seq, n_head, *arrays):
    (inner, groups, gate, step, bias, decay, taps_i, taps_g, gain, query, key, value, segs, mproj, aproj) = arrays
    tokens, channels = inner.shape
    half = channels // 2
    wide = groups.shape[1]
    out_width = mproj.shape[1] // n_head
    chunks = half // LANES
    vmem = pl.BlockSpec(memory_space=pltpu.VMEM)
    hbm = pl.BlockSpec(memory_space=pltpu.HBM)
    dma = pltpu.SemaphoreType.DMA
    scratch = [
        pltpu.VMEM((3, 1, tokens), segs.dtype),
        pltpu.VMEM((2, *step.shape), F32),
        pltpu.VMEM(bias.shape, F32),
        pltpu.VMEM(decay.shape, F32),
        pltpu.VMEM((taps_i.shape[0], half), F32),
        pltpu.VMEM(taps_g.shape, F32),
        pltpu.VMEM(gain.shape, F32),
        pltpu.VMEM(query.shape, BF16),
        pltpu.VMEM(gate.shape, BF16),
        pltpu.VMEM((2, tokens, half), BF16),
        pltpu.VMEM((2, tokens, wide), BF16),
        pltpu.VMEM((2, RIM, half), BF16),
        pltpu.VMEM((2, RIM, wide), BF16),
        pltpu.VMEM((n_seq, 2, tokens + RIM, HD), BF16),
        pltpu.VMEM((2, RIM + tokens, half), F32),
        pltpu.VMEM((2, RIM + tokens, wide), F32),
        pltpu.VMEM((2, tokens, half), BF16),
        pltpu.VMEM((2, tokens, STATE_SIZE), BF16),
        pltpu.VMEM((2, tokens, STATE_SIZE), BF16),
        pltpu.VMEM((2 * tokens, half), F32),
        pltpu.VMEM((STATE_SIZE, half), F32),
        *[pltpu.VMEM((PIECES * chunks, STATE_SIZE // PIECES, LANES), BF16) for _ in range(2)],
        *[pltpu.VMEM((chunks, tokens, LANES), BF16) for _ in range(2)],
        pltpu.VMEM((tokens, channels + query.shape[1]), BF16),
        pltpu.VMEM(mproj.shape, BF16),
        pltpu.VMEM(aproj.shape, BF16),
        pltpu.VMEM((6, tokens, out_width // 2), BF16),
        pltpu.VMEM((6, tokens, out_width // 2), BF16),
        pltpu.VMEM((n_seq, query.shape[1] // HD * tokens, tokens), F32),
        *[pltpu.VMEM((query.shape[1] // HD * tokens, n), F32) for n in (tokens, tokens, HD)],
        pltpu.SemaphoreType.REGULAR((n_seq,)),
        dma((13,)),
        dma((2,)),
        dma((chunks,)),
        dma((chunks,)),
        dma((4,)),
        dma((4,)),
        dma((2,)),
        dma((2, 2)),
        dma((2, 2)),
        dma((3,)),
        dma((3,)),
        *[dma((n_seq,)) for _ in range(5)],
        *[dma((PIECES * chunks,)) for _ in range(2)],
        *[dma((chunks,)) for _ in range(2)],
        dma((6,)),
        dma((6,)),
    ]
    return pl.pallas_call(
        functools.partial(kernel, n_seq, n_head),
        out_shape=jax.ShapeDtypeStruct((tokens, out_width), BF16),
        in_specs=[hbm] * 15,
        out_specs=vmem,
        scratch_shapes=scratch,
        compiler_params=pltpu.CompilerParams(
            collective_id=0, has_side_effects=True, vmem_limit_bytes=64 * 2**20
        ),
        name="mixer",
    )(*arrays)


def solution(mesh):
    placed = (
        P("seq", "head"),
        P("seq", None),
        P("seq", "head"),
        P("head", "seq"),
        P("head"),
        P("head"),
        P(None, "head"),
        P(),
        P("head"),
        P("seq", "head"),
        P("seq", None),
        P("seq", None),
        P("seq"),
        P("head", None),
        P("head", None),
    )
    return jax.shard_map(
        functools.partial(shards, mesh.shape["seq"], mesh.shape["head"]),
        mesh=mesh,
        in_specs=placed,
        out_specs=P("seq", "head"),
        check_vma=False,
    )
```

```python
import functools
import math

import jax
import jax.numpy as jnp
from jax import lax
from jax.experimental import pallas as pl
from jax.experimental.pallas import tpu as pltpu
from jax.sharding import PartitionSpec as P

HEAD_CHANNELS = 64
STATE_SIZE = 256
QH = 8
KVH = 2
HD = 128
LANES = 128
RIM = 16
PIECES = 4
F32 = jnp.float32
BF16 = jnp.bfloat16
MESH = pl.DeviceIdType.MESH


def dot(a, b, contract):
    return lax.dot_general(a, b, ((contract[:1], contract[1:]), ((), ())), preferred_element_type=F32)


def iota(shape, axis):
    return lax.broadcasted_iota(jnp.int32, shape, axis)


def column(row):
    n = row.shape[1]
    eye = iota((n, n), 0) == iota((n, n), 1)
    return jnp.sum(jnp.where(eye, jnp.broadcast_to(row, (n, n)), 0.0), axis=1, keepdims=True)


def thirds(a):
    high = a.astype(BF16).astype(F32)
    rest = a - high
    middle = rest.astype(BF16).astype(F32)
    return jnp.concatenate([high, middle, rest - middle], axis=0).astype(BF16)


def to_columns(rows):
    n = rows.shape[0]
    pick = (iota((3 * n, n), 0) % n == iota((3 * n, n), 1)).astype(BF16)
    return dot(thirds(rows), pick, (0, 0))


def kernel(
    n_seq,
    n_head,
    inner_hbm,
    groups_hbm,
    gate_hbm,
    step_hbm,
    bias_hbm,
    decay_hbm,
    taps_inner_hbm,
    taps_groups_hbm,
    gain_hbm,
    query_hbm,
    key_hbm,
    value_hbm,
    segs_hbm,
    mamba_proj_hbm,
    attn_proj_hbm,
    out_ref,
    segs_ref,
    step_in,
    bias_ref,
    decay_ref,
    taps_inner_ref,
    taps_groups_ref,
    gain_ref,
    query_ref,
    gate_ref,
    x_in,
    g_in,
    rim_x,
    rim_g,
    kv,
    pad_x,
    pad_g,
    conv_x,
    conv_b,
    conv_c,
    y_ref,
    state,
    e_send,
    e_recv,
    f_send,
    f_recv,
    both,
    mproj,
    aproj,
    rs_send,
    rs_recv,
    scores_ref,
    top_ref,
    total_ref,
    summed_ref,
    ready,
    load_sem,
    weight_sem,
    x_ss,
    x_rs,
    g_ss,
    g_rs,
    step_sem,
    rim_ss,
    rim_rs,
    seg_ss,
    seg_rs,
    kv_ss,
    across_ss,
    kv_rs,
    share_ss,
    share_rs,
    e_ss,
    e_rs,
    f_ss,
    f_rs,
    rs_ss,
    rs_rs,
):
    tokens, channels = gate_ref.shape
    heads = step_in.shape[1]
    half = channels // 2
    few = heads // 2
    chunks = half // LANES
    wide = groups_hbm.shape[1]
    taps = taps_inner_ref.shape[0]
    depth = STATE_SIZE // PIECES
    heads_here = query_ref.shape[1] // HD
    me = lax.axis_index("seq")
    mine = lax.axis_index("head")
    pair, side = me // 2, me % 2
    other = 1 - side
    last_pair = n_seq // 2 - 1
    partner = me + 1 - 2 * side
    upper = lax.min(me + 2, n_seq - 1)
    lower = lax.max(me - 2, 0)
    following = lax.min(me + 1, n_seq - 1)
    previous = lax.max(me - 1, 0)
    core = mine % 2
    sibling = mine + 1 - 2 * core
    opposite = (mine + 2) % n_head
    opposite_sibling = (sibling + 2) % n_head
    has_upper, has_lower = pair < last_pair, pair > 0

    def at_seq(s):
        return (s, mine)

    def at_head(h):
        return (me, h)

    def remote(src, dst, ss, rs, target):
        return pltpu.make_async_remote_copy(src, dst, ss, rs, device_id=target, device_id_type=MESH)

    def part(which, c):
        return pl.ds(pl.multiple_of(which * half + c * LANES, LANES), LANES)

    def side_half(which):
        return pl.ds(pl.multiple_of(which * half, LANES), half)

    def core_cols(kind):
        return pl.ds(kind * STATE_SIZE, STATE_SIZE)

    kv_head = mine * heads_here // (QH // KVH)
    kv_cols = pl.ds(pl.multiple_of(kv_head * HD, HD), HD)
    body = pl.ds(0, tokens)

    weights = [
        pltpu.make_async_copy(mamba_proj_hbm, mproj, weight_sem.at[0]),
        pltpu.make_async_copy(attn_proj_hbm, aproj, weight_sem.at[1]),
    ]
    loads = [
        pltpu.make_async_copy(src, dst, load_sem.at[i])
        for i, (src, dst) in enumerate(
            (
                (segs_hbm, segs_ref.at[1 + side, 0]),
                (key_hbm.at[:, kv_cols], kv.at[me, 0, body]),
                (value_hbm.at[:, kv_cols], kv.at[me, 1, body]),
                (groups_hbm, g_in.at[side]),
                (taps_groups_hbm, taps_groups_ref),
                (inner_hbm.at[:, side_half(side)], x_in.at[side]),
                (taps_inner_hbm.at[:, side_half(side)], taps_inner_ref),
                (step_hbm, step_in.at[side]),
                (bias_hbm, bias_ref),
                (decay_hbm, decay_ref),
                (query_hbm, query_ref),
                (gate_hbm, gate_ref),
                (gain_hbm, gain_ref),
            )
        )
    ]

    barrier = pltpu.get_barrier_semaphore()

    def hello(target):
        pl.semaphore_signal(barrier, inc=1, device_id=target, device_id_type=MESH)

    hello(at_seq(partner))
    hello(at_head(sibling))
    hello(at_head(opposite))

    def hello_later(s, _):
        hello(at_seq(me + 2 * s))
        return 0

    lax.fori_loop(1, last_pair - pair + 1, hello_later, 0)

    @pl.when(has_upper & (side == 1))
    def _():
        hello(at_seq(following))

    for w in loads:
        w.start()
    pl.semaphore_wait(barrier, 3 + pair + jnp.where(has_lower, other, 0))

    def answer(k):
        pl.semaphore_signal(ready.at[me], inc=1, device_id=at_seq(k), device_id_type=MESH)

    @pl.when(has_lower & (side == 0))
    def _():
        answer(previous)

    lax.fori_loop(1, pair + 1, lambda s, _: answer(me - 2 * s) or 0, 0)

    tail_rows = pl.ds(tokens - RIM, RIM)

    def rim_copies(kind, target, slot, which):
        return [
            remote(
                inner_hbm.at[tail_rows, side_half(which)], rim_x.at[slot], rim_ss.at[kind, 0], rim_rs.at[slot, 0], at_seq(target)
            ),
            remote(groups_hbm.at[tail_rows, :], rim_g.at[slot], rim_ss.at[kind, 1], rim_rs.at[slot, 1], at_seq(target)),
        ]

    def rim_next():
        return rim_copies(0, following, other, other)

    def rim_skip():
        return rim_copies(1, upper, 0, side)

    def group_copy(block, kind):
        at = core_cols(kind)
        return remote(groups_hbm.at[:, at], g_in.at[block, :, at], g_ss.at[kind], g_rs.at[kind], at_seq(partner))

    def x_copy(block, c):
        return remote(
            inner_hbm.at[:, part(other, c)],
            x_in.at[block, :, pl.ds(c * LANES, LANES)],
            x_ss.at[c],
            x_rs.at[c],
            at_seq(partner),
        )

    def step_copy(block):
        return remote(step_hbm, step_in.at[block], step_sem.at[0], step_sem.at[1], at_seq(partner))

    def seg_copy(kind, target, dst):
        return remote(segs_hbm, segs_ref.at[dst, 0], seg_ss.at[kind], seg_rs.at[dst], at_seq(target))

    step_copy(side).start()
    seg_copy(0, partner, 1 + side).start()

    group_copy(side, 0).start()
    x_copy(side, 0).start()

    @pl.when(side == 0)
    def _():
        for c in rim_next():
            c.start()

    for c in range(1, chunks):
        x_copy(side, c).start()
    group_copy(side, 1).start()

    def kv_copy(b, k):
        return remote(kv.at[b, core], kv.at[b, core], kv_ss.at[k], kv_rs.at[b], at_seq(k))

    def kv_share(b):
        return remote(kv.at[b, core], kv.at[b, core], share_ss.at[b], share_rs.at[b], at_head(sibling))

    def kv_across(b):
        return remote(kv.at[b, core], kv.at[b, core], across_ss.at[b], kv_rs.at[b], at_seq(partner))

    def pass_on(s, _):
        kv_copy(me - 2 * s, partner).wait_recv()
        kv_across(me - 2 * s).start()
        kv_share(me - 2 * s).start()
        return 0

    def pass_across(s, _):
        kv_across(partner - 2 * s).wait_recv()
        kv_share(partner - 2 * s).start()
        return 0

    def conv_flags(b, before):
        now = segs_of(b + 1)
        both_blocks = jnp.concatenate([before, now], axis=1)
        row = iota((8, tokens), 0)
        flags = now
        for back in range(1, taps):
            kept = (pltpu.roll(both_blocks, back, 1)[:, tokens:] == now).astype(F32)
            flags = jnp.where(row == back, kept, flags)
        eye = (iota((8, 8), 0) == iota((8, 8), 1)).astype(BF16)
        return dot(flags.astype(BF16), eye, (0, 0))

    def keeps_of(flags, n):
        return [jnp.broadcast_to(flags[:n, back : back + 1], (n, LANES)) > 0.5 for back in range(taps - 1, 0, -1)]

    def conv(pad, b, cols, keeps, weight_ref, n):
        acc = weight_ref[taps - 1 : taps, cols] * pad[b, RIM : RIM + n, cols]
        for k in range(taps - 1):
            first = RIM - (taps - 1) + k
            term = weight_ref[k : k + 1, cols] * pad[b, first : first + n, cols]
            acc = acc + jnp.where(keeps[k], term, 0.0)
        return jax.nn.silu(acc).astype(BF16)

    def conv_groups(b, kind, keeps, n):
        out = (conv_b, conv_c)[kind]
        for c in range(0, STATE_SIZE, LANES):
            at = slice(kind * STATE_SIZE + c, kind * STATE_SIZE + c + LANES)
            out[b, 0:n, c : c + LANES] = conv(pad_g, b, at, keeps, taps_groups_ref, n)

    def conv_inner(b, c, keeps, n):
        at = slice(c * LANES, (c + 1) * LANES)
        conv_x[b, 0:n, at] = conv(pad_x, b, at, keeps, taps_inner_ref, n)

    def rim_arrived(slot):
        for c in rim_copies(0, partner, slot, slot):
            c.wait_recv()

    def segs_of(at):
        return jnp.broadcast_to(segs_ref[at].astype(F32), (8, tokens))

    for w in (loads[0], *loads[3:7]):
        w.wait()
    pad_g[side, 0:RIM, :] = jnp.zeros((RIM, wide), F32)
    pad_x[side, 0:RIM, :] = jnp.zeros((RIM, half), F32)
    pad_g[side, RIM:, :] = g_in[side].astype(F32)
    pad_x[side, RIM:, :] = x_in[side].astype(F32)
    own_flags = conv_flags(side, jnp.full((8, tokens), -1.0, F32))
    own_keeps = keeps_of(own_flags, tokens)
    conv_groups(side, 0, own_keeps, tokens)

    own_segs = jnp.broadcast_to(segs_ref[1 + side].astype(F32), (RIM, tokens)).astype(BF16)
    kv[me, 0, pl.ds(tokens, RIM), :] = own_segs
    kv[me, 1, pl.ds(tokens, RIM), :] = own_segs
    loads[1].wait()
    loads[2].wait()

    @pl.when(side == 0)
    def _():
        kv_across(me).start()

    @pl.when(has_upper)
    def _():
        pl.semaphore_wait(ready.at[upper], 1)

    @pl.when(has_upper & (side == 1))
    def _():
        pl.semaphore_wait(ready.at[following], 1)
        seg_copy(1, following, 0).start()
        seg_copy(2, upper, 0).start()
        for c in rim_skip():
            c.start()
        for c in rim_next():
            c.start()

    @pl.when(has_upper)
    def _():
        kv_copy(me, upper).start()

    for c in range(chunks):
        conv_inner(side, c, own_keeps, tokens)

    for w in loads[7:10]:
        w.wait()
    step_copy(other).wait_recv()
    seg_copy(0, partner, 1 + other).wait_recv()
    bias = column(bias_ref[...].reshape(1, heads))
    rates = jnp.exp(column(decay_ref[...].reshape(1, heads)))
    on_left = side == 0

    def mine_of(a):
        kept = jnp.where(on_left, a[:few], a[few:])
        return jnp.concatenate([kept, jnp.zeros((8 - few, a.shape[1]), F32)], axis=0)

    raw = mine_of(jnp.concatenate([step_in[0], step_in[1]], axis=1) + bias)
    steps = jnp.maximum(raw, 0.0) + jnp.log1p(jnp.exp(-jnp.abs(raw)))
    span = 2 * tokens
    row_t, col_t = iota((span, span), 0), iota((span, span), 1)
    upto = (row_t <= col_t).astype(BF16)
    sums = dot(thirds(-steps * mine_of(rates)), upto, (1, 0))
    cumul = sums[0:8] + sums[8:16] + sums[16:24]
    total = cumul[:, span - 1 : span]
    segs_rows8 = jnp.concatenate([segs_of(1), segs_of(2)], axis=1)
    last_seg = segs_rows8[:, span - 1 : span]
    weigh = jnp.where(segs_rows8 == last_seg, jnp.exp(total - cumul), 0.0) * steps
    cols = to_columns(jnp.concatenate([cumul, weigh, jnp.exp(cumul), segs_rows8], axis=0))
    left = iota((span, LANES), 1) < HEAD_CHANNELS

    def two_heads(base, c):
        a, b = base + 2 * c, base + 2 * c + 1
        return jnp.where(left, cols[:, a : a + 1], cols[:, b : b + 1])

    group_copy(other, 0).wait_recv()

    def send_far(s, _):
        pl.semaphore_wait(ready.at[me + 2 * s], 1)
        kv_copy(me, me + 2 * s).start()
        return 0

    lax.fori_loop(2, last_pair - pair + 1, send_far, 0)

    other_keeps = keeps_of(conv_flags(other, jnp.full((8, tokens), -1.0, F32)), tokens)
    pad_g[other, 0:RIM, :] = jnp.zeros((RIM, wide), F32)
    pad_x[other, 0:RIM, :] = jnp.zeros((RIM, half), F32)
    pad_g[other, RIM:, 0:STATE_SIZE] = g_in[other, :, 0:STATE_SIZE].astype(F32)
    conv_groups(other, 0, other_keeps, tokens)

    def conv_other(c):
        lanes = slice(c * LANES, (c + 1) * LANES)
        x_copy(other, c).wait_recv()
        pad_x[other, RIM:, lanes] = x_in[other, :, lanes].astype(F32)
        conv_inner(other, c, other_keeps, tokens)

    conv_other(0)

    @pl.when(has_lower)
    def _():
        seg_copy(0, partner, 0).wait_recv()
        rim_arrived(0)

    @pl.when(pair == 0)
    def _():
        segs_ref[0] = jnp.full((1, tokens), -1, jnp.int32)
        rim_x[0] = jnp.zeros_like(rim_x[0])
        rim_g[0] = jnp.zeros_like(rim_g[0])

    @pl.when(side == 1)
    def _():
        rim_arrived(1)

    @pl.when(side == 0)
    def _():
        rim_x[1] = x_in[0, tokens - RIM :, :]
        rim_g[1] = g_in[0, tokens - RIM :, :]

    first_keeps = []
    for b in range(2):
        pad_g[b, 0:RIM, :] = rim_g[b].astype(F32)
        pad_x[b, 0:RIM, :] = rim_x[b].astype(F32)
        first_keeps.append(keeps_of(conv_flags(b, segs_of(b)), RIM))
        conv_groups(b, 0, first_keeps[b], RIM)

    read_b = conv_b[...].reshape(span, STATE_SIZE)
    across_b = read_b.T

    def hop(src, dst, ss, rs, c, target):
        return remote(src.at[c], dst.at[c], ss.at[c], rs.at[c], at_seq(target))

    def e_hop(i, target):
        return hop(e_send, e_recv, e_ss, e_rs, i, target)

    for c in range(chunks):
        if c > 0:
            conv_other(c)
        for b in range(2):
            conv_inner(b, c, first_keeps[b], RIM)
        lanes = slice(c * LANES, (c + 1) * LANES)
        x = conv_x[:, :, lanes].reshape(span, LANES).astype(F32)
        state[:, lanes] = dot(across_b, (two_heads(8, c) * x).astype(BF16), (1, 0))

        @pl.when(pair == 0)
        def _():
            for r in range(PIECES):
                i = PIECES * c + r
                e_send[i] = state[r * depth : (r + 1) * depth, lanes].astype(BF16)
                e_hop(i, upper).start()

    lax.fori_loop(1, pair + 1, pass_on, 0)
    group_copy(other, 1).wait_recv()
    pad_g[side, 0:RIM, STATE_SIZE:] = jnp.zeros((RIM, STATE_SIZE), F32)
    conv_groups(side, 1, own_keeps, tokens)
    pad_g[side, 0:RIM, STATE_SIZE:] = rim_g[side, :, STATE_SIZE:].astype(F32)

    prev_last = segs_of(0)[:, tokens - 1 : tokens]
    spread = iota((8, half), 1) // HEAD_CHANNELS == iota((8, half), 0)
    crossing_pair = jnp.where(last_seg == prev_last, jnp.exp(total), 0.0)
    through = jnp.sum(jnp.where(spread, crossing_pair, 0.0), axis=0, keepdims=True)
    joined = cols[:, 24:25] == prev_last[0:1]
    pad_g[other, RIM:, STATE_SIZE:] = g_in[other, :, STATE_SIZE:].astype(F32)
    conv_groups(other, 1, other_keeps, tokens)
    for b in range(2):
        conv_groups(b, 1, first_keeps[b], RIM)
    read_c = conv_c[...].reshape(span, STATE_SIZE)

    for w in weights:
        w.start()

    for w in loads[10:]:
        w.wait()
    scale = 1.0 / math.sqrt(HD)
    queries = jnp.concatenate([query_ref[:, h * HD : (h + 1) * HD] for h in range(heads_here)], axis=0)
    rows = heads_here * tokens
    segs_q = jnp.concatenate([own_flags[:, 0:1]] * heads_here, axis=0)
    token_q = jnp.concatenate([iota((tokens, 1), 0)] * heads_here, axis=0)
    top_ref[...] = jnp.full((rows, tokens), -jnp.inf, F32)
    total_ref[...] = jnp.zeros((rows, tokens), F32)
    summed_ref[...] = jnp.zeros((rows, HD), F32)

    def attend(k):
        @pl.when(k != me)
        def _():
            kv_share(k).wait_recv()

        scores = dot(queries, kv[k, 0, 0:tokens, :], (1, 1)) * scale
        segs_k = kv[k, 0, tokens:, :].astype(F32)[0:1, :tokens]
        allowed = (segs_k == segs_q) & (iota((rows, tokens), 1) + (k - me) * tokens <= token_q)
        scores = jnp.where(allowed, scores, -jnp.inf)
        scores_ref[k] = scores
        top_ref[...] = jnp.maximum(top_ref[...], scores)

    same_head = (iota((2 * LANES, LANES), 0) % LANES // HEAD_CHANNELS == iota((2 * LANES, LANES), 1) // HEAD_CHANNELS).astype(
        BF16
    )
    gain_row = gain_ref[...].reshape(1, channels)
    gains = [
        jnp.where(on_left, gain_row[:, :half], gain_row[:, half:]),
        jnp.where(on_left, gain_row[:, half:], gain_row[:, :half]),
    ]

    def norm(which, c, gain, y):
        at = part(which, c)
        gated = y * jax.nn.silu(gate_ref[:, at].astype(F32))
        square = gated * gated
        high = square.astype(BF16)
        parts = jnp.concatenate([high, (square - high.astype(F32)).astype(BF16)], axis=1)
        mean_square = dot(parts, same_head, (1, 0)) * (1.0 / HEAD_CHANNELS)
        normed = gated * lax.rsqrt(mean_square + 1e-05) * gain[:, c * LANES : (c + 1) * LANES]
        both[:, at] = normed.astype(BF16)

    def f_hop(c):
        return hop(f_send, f_recv, f_ss, f_rs, c, partner)

    @pl.when(pair == 0)
    def _():
        e_recv[...] = jnp.zeros_like(e_recv)

    live = (cols[:, 24:25] == segs_rows8[0:1]) & (row_t >= col_t)
    crossing = dot(read_c, across_b, (1, 0))
    for c in range(chunks):
        lanes = slice(c * LANES, (c + 1) * LANES)
        x = conv_x[:, :, lanes].reshape(span, LANES)
        got = []
        for h in (2 * c, 2 * c + 1):
            halves = []
            for rows_of, width in ((slice(0, tokens), tokens), (slice(tokens, span), span)):
                gap = cols[rows_of, h : h + 1] - cumul[h : h + 1, :width]
                decays = jnp.exp(jnp.where(live[rows_of, :width], gap, -jnp.inf))
                mixing = (crossing[rows_of, :width] * decays * steps[h : h + 1, :width]).astype(BF16)
                halves.append(dot(mixing, x[:width], (1, 0)))
            got.append(jnp.concatenate(halves, axis=0))
        y_ref[:, lanes] = jnp.where(left, got[0], got[1])

    def attend_line():
        lax.fori_loop(0, pair + 1, lambda s, _: attend(me - 2 * s) or 0, 0)
        lax.fori_loop(other, pair + 1, pass_across, 0)

    def attend_rest():
        lax.fori_loop(other, pair + 1, lambda s, _: attend(partner - 2 * s) or 0, 0)
        top = jnp.max(top_ref[...], axis=1, keepdims=True)

        def add(k, _):
            w = jnp.exp(scores_ref[k] - top)
            total_ref[...] += w
            summed_ref[...] += dot(w.astype(BF16), kv[k, 1, 0:tokens, :], (1, 0))
            return 0

        lax.fori_loop(0, me + 1, add, 0)
        attended = (summed_ref[...] / jnp.sum(total_ref[...], axis=1, keepdims=True)).astype(BF16)
        for h in range(heads_here):
            both[:, channels + h * HD : channels + (h + 1) * HD] = attended[h * tokens : (h + 1) * tokens]

    pl.when(pair == last_pair)(attend_line)
    for c in range(chunks):
        lanes = slice(c * LANES, (c + 1) * LANES)

        @pl.when(has_lower)
        def _():
            for r in range(PIECES):
                i = PIECES * c + r
                e_hop(i, partner).wait_recv()

                @pl.when(has_upper)
                def _():
                    enters = e_recv[i].astype(F32)
                    e_send[i] = (through[:, lanes] * enters + state[r * depth : (r + 1) * depth, lanes]).astype(BF16)
                    e_hop(i, upper).start()

        enters = jnp.concatenate([e_recv[PIECES * c + r] for r in range(PIECES)], axis=0)
        carried = jnp.where(joined, two_heads(16, c), 0.0) * dot(read_c, enters, (1, 0))
        y = y_ref[:, lanes] + carried
        f_send[c] = jnp.where(on_left, y[tokens:], y[:tokens]).astype(BF16)
        f_hop(c).start()
        norm(side, c, gains[0], jnp.where(on_left, y[:tokens], y[tokens:]))

    pl.when(pair < last_pair)(attend_line)
    attend_rest()
    for c in range(chunks):
        f_hop(c).wait_recv()
        norm(other, c, gains[1], f_recv[c].astype(F32))

    for w in weights:
        w.wait()
    width = out_ref.shape[1]

    def product(j, part_of):
        at = pl.ds(pl.multiple_of(j * width + part_of * (width // 2), LANES), width // 2)
        return dot(both[:, :channels], mproj[:, at], (1, 0)) + dot(both[:, channels:], aproj[:, at], (1, 0))

    def rs_copy(i, target):
        return remote(rs_send.at[i], rs_recv.at[i], rs_ss.at[i], rs_rs.at[i], at_head(target))

    to_pair = [rs_copy(h, sibling) for h in range(2)]
    to_sibling = [rs_copy(2 + h, sibling) for h in range(2)]
    to_opposite = [rs_copy(4 + h, opposite) for h in range(2)]
    for h in range(2):
        rs_send[h] = product(opposite_sibling, h).astype(BF16)
        to_pair[h].start()
    for h in range(2):
        away = product(opposite, h)
        to_pair[h].wait_recv()
        rs_send[4 + h] = (away + rs_recv[h].astype(F32)).astype(BF16)
        to_opposite[h].start()
    for h in range(2):
        rs_send[2 + h] = product(sibling, h).astype(BF16)
        to_sibling[h].start()
    for h in range(2):
        result = product(mine, h)
        to_sibling[h].wait_recv()
        result = result + rs_recv[2 + h].astype(F32)
        to_opposite[h].wait_recv()
        out_ref[:, h * (width // 2) : (h + 1) * (width // 2)] = (result + rs_recv[4 + h].astype(F32)).astype(BF16)

    for copy in (*to_pair, *to_sibling, *to_opposite, step_copy(side)):
        copy.wait_send()
    for c in range(chunks):
        x_copy(side, c).wait_send()
        f_hop(c).wait_send()
    for kind in range(2):
        group_copy(side, kind).wait_send()
    seg_copy(0, partner, 1 + side).wait_send()

    @pl.when(me < n_seq - 1)
    def _():
        for c in rim_next():
            c.wait_send()

    @pl.when(has_upper & (side == 1))
    def _():
        for c in rim_skip():
            c.wait_send()
        seg_copy(1, following, 0).wait_send()
        seg_copy(2, upper, 0).wait_send()

    @pl.when(has_upper)
    def _():
        for i in range(PIECES * chunks):
            e_hop(i, upper).wait_send()

    def sent_kv(s, _):
        kv_copy(me, me + 2 * s).wait_send()
        return 0

    lax.fori_loop(1, last_pair - pair + 1, sent_kv, 0)

    def sent_on(s, _):
        kv_across(me - 2 * s).wait_send()
        kv_share(me - 2 * s).wait_send()
        return 0

    lax.fori_loop(1, pair + 1, sent_on, 0)

    @pl.when(side == 0)
    def _():
        kv_across(me).wait_send()

    def sent_share(s, _):
        kv_share(partner - 2 * s).wait_send()
        return 0

    lax.fori_loop(other, pair + 1, sent_share, 0)


def shards(n_seq, n_head, *arrays):
    (inner, groups, gate, step, bias, decay, taps_i, taps_g, gain, query, key, value, segs, mproj, aproj) = arrays
    tokens, channels = inner.shape
    half = channels // 2
    wide = groups.shape[1]
    out_width = mproj.shape[1] // n_head
    chunks = half // LANES
    vmem = pl.BlockSpec(memory_space=pltpu.VMEM)
    hbm = pl.BlockSpec(memory_space=pltpu.HBM)
    dma = pltpu.SemaphoreType.DMA
    scratch = [
        pltpu.VMEM((3, 1, tokens), segs.dtype),
        pltpu.VMEM((2, *step.shape), F32),
        pltpu.VMEM(bias.shape, F32),
        pltpu.VMEM(decay.shape, F32),
        pltpu.VMEM((taps_i.shape[0], half), F32),
        pltpu.VMEM(taps_g.shape, F32),
        pltpu.VMEM(gain.shape, F32),
        pltpu.VMEM(query.shape, BF16),
        pltpu.VMEM(gate.shape, BF16),
        pltpu.VMEM((2, tokens, half), BF16),
        pltpu.VMEM((2, tokens, wide), BF16),
        pltpu.VMEM((2, RIM, half), BF16),
        pltpu.VMEM((2, RIM, wide), BF16),
        pltpu.VMEM((n_seq, 2, tokens + RIM, HD), BF16),
        pltpu.VMEM((2, RIM + tokens, half), F32),
        pltpu.VMEM((2, RIM + tokens, wide), F32),
        pltpu.VMEM((2, tokens, half), BF16),
        pltpu.VMEM((2, tokens, STATE_SIZE), BF16),
        pltpu.VMEM((2, tokens, STATE_SIZE), BF16),
        pltpu.VMEM((2 * tokens, half), F32),
        pltpu.VMEM((STATE_SIZE, half), F32),
        *[pltpu.VMEM((PIECES * chunks, STATE_SIZE // PIECES, LANES), BF16) for _ in range(2)],
        *[pltpu.VMEM((chunks, tokens, LANES), BF16) for _ in range(2)],
        pltpu.VMEM((tokens, channels + query.shape[1]), BF16),
        pltpu.VMEM(mproj.shape, BF16),
        pltpu.VMEM(aproj.shape, BF16),
        pltpu.VMEM((6, tokens, out_width // 2), BF16),
        pltpu.VMEM((6, tokens, out_width // 2), BF16),
        pltpu.VMEM((n_seq, query.shape[1] // HD * tokens, tokens), F32),
        *[pltpu.VMEM((query.shape[1] // HD * tokens, n), F32) for n in (tokens, tokens, HD)],
        pltpu.SemaphoreType.REGULAR((n_seq,)),
        dma((13,)),
        dma((2,)),
        dma((chunks,)),
        dma((chunks,)),
        dma((2,)),
        dma((2,)),
        dma((2,)),
        dma((2, 2)),
        dma((2, 2)),
        dma((3,)),
        dma((3,)),
        *[dma((n_seq,)) for _ in range(5)],
        *[dma((PIECES * chunks,)) for _ in range(2)],
        *[dma((chunks,)) for _ in range(2)],
        dma((6,)),
        dma((6,)),
    ]
    return pl.pallas_call(
        functools.partial(kernel, n_seq, n_head),
        out_shape=jax.ShapeDtypeStruct((tokens, out_width), BF16),
        in_specs=[hbm] * 15,
        out_specs=vmem,
        scratch_shapes=scratch,
        compiler_params=pltpu.CompilerParams(
            collective_id=0, has_side_effects=True, vmem_limit_bytes=64 * 2**20
        ),
        name="mixer",
    )(*arrays)


def solution(mesh):
    placed = (
        P("seq", "head"),
        P("seq", None),
        P("seq", "head"),
        P("head", "seq"),
        P("head"),
        P("head"),
        P(None, "head"),
        P(),
        P("head"),
        P("seq", "head"),
        P("seq", None),
        P("seq", None),
        P("seq"),
        P("head", None),
        P("head", None),
    )
    return jax.shard_map(
        functools.partial(shards, mesh.shape["seq"], mesh.shape["head"]),
        mesh=mesh,
        in_specs=placed,
        out_specs=P("seq", "head"),
        check_vma=False,
    )
```

```python
import functools
import math

import jax
import jax.numpy as jnp
from jax import lax
from jax.experimental import pallas as pl
from jax.experimental.pallas import tpu as pltpu
from jax.sharding import PartitionSpec as P

HEAD_CHANNELS = 64
STATE_SIZE = 256
QH = 8
KVH = 2
HD = 128
LANES = 128
RIM = 16
PIECES = 4
CUTS = 4
F32 = jnp.float32
BF16 = jnp.bfloat16
MESH = pl.DeviceIdType.MESH


def dot(a, b, contract):
    return lax.dot_general(a, b, ((contract[:1], contract[1:]), ((), ())), preferred_element_type=F32)


def iota(shape, axis):
    return lax.broadcasted_iota(jnp.int32, shape, axis)


def column(row):
    n = row.shape[1]
    eye = iota((n, n), 0) == iota((n, n), 1)
    return jnp.sum(jnp.where(eye, jnp.broadcast_to(row, (n, n)), 0.0), axis=1, keepdims=True)


def thirds(a):
    high = a.astype(BF16).astype(F32)
    rest = a - high
    middle = rest.astype(BF16).astype(F32)
    return jnp.concatenate([high, middle, rest - middle], axis=0).astype(BF16)


def to_columns(rows):
    n = rows.shape[0]
    pick = (iota((3 * n, n), 0) % n == iota((3 * n, n), 1)).astype(BF16)
    return dot(thirds(rows), pick, (0, 0))


def kernel(
    n_seq,
    n_head,
    inner_hbm,
    groups_hbm,
    gate_hbm,
    step_hbm,
    bias_hbm,
    decay_hbm,
    taps_inner_hbm,
    taps_groups_hbm,
    gain_hbm,
    query_hbm,
    key_hbm,
    value_hbm,
    segs_hbm,
    mamba_proj_hbm,
    attn_proj_hbm,
    out_ref,
    segs_ref,
    step_in,
    bias_ref,
    decay_ref,
    taps_inner_ref,
    taps_groups_ref,
    gain_ref,
    query_ref,
    gate_ref,
    x_in,
    g_in,
    rim_x,
    rim_g,
    kv,
    pad_x,
    pad_g,
    conv_x,
    conv_b,
    conv_c,
    y_ref,
    state,
    e_send,
    e_recv,
    f_send,
    f_recv,
    both,
    mproj,
    aproj,
    rs_send,
    rs_recv,
    scores_ref,
    top_ref,
    total_ref,
    summed_ref,
    ready,
    load_sem,
    weight_sem,
    x_ss,
    x_rs,
    g_ss,
    g_rs,
    step_sem,
    rim_ss,
    rim_rs,
    seg_ss,
    seg_rs,
    kv_ss,
    across_ss,
    kv_rs,
    share_ss,
    share_rs,
    e_ss,
    e_rs,
    f_ss,
    f_rs,
    rs_ss,
    rs_rs,
):
    tokens, channels = gate_ref.shape
    heads = step_in.shape[1]
    half = channels // 2
    few = heads // 2
    chunks = half // LANES
    wide = groups_hbm.shape[1]
    taps = taps_inner_ref.shape[0]
    depth = STATE_SIZE // PIECES
    heads_here = query_ref.shape[1] // HD
    me = lax.axis_index("seq")
    mine = lax.axis_index("head")
    pair, side = me // 2, me % 2
    other = 1 - side
    last_pair = n_seq // 2 - 1
    partner = me + 1 - 2 * side
    upper = lax.min(me + 2, n_seq - 1)
    lower = lax.max(me - 2, 0)
    following = lax.min(me + 1, n_seq - 1)
    previous = lax.max(me - 1, 0)
    core = mine % 2
    sibling = mine + 1 - 2 * core
    opposite = (mine + 2) % n_head
    opposite_sibling = (sibling + 2) % n_head
    has_upper, has_lower = pair < last_pair, pair > 0

    def at_seq(s):
        return (s, mine)

    def at_head(h):
        return (me, h)

    def remote(src, dst, ss, rs, target):
        return pltpu.make_async_remote_copy(src, dst, ss, rs, device_id=target, device_id_type=MESH)

    def part(which, c):
        return pl.ds(pl.multiple_of(which * half + c * LANES, LANES), LANES)

    def side_half(which):
        return pl.ds(pl.multiple_of(which * half, LANES), half)

    def core_cols(kind):
        return pl.ds(kind * STATE_SIZE, STATE_SIZE)

    kv_head = mine * heads_here // (QH // KVH)
    kv_cols = pl.ds(pl.multiple_of(kv_head * HD, HD), HD)
    body = pl.ds(0, tokens)

    weights = [
        pltpu.make_async_copy(mamba_proj_hbm, mproj, weight_sem.at[0]),
        pltpu.make_async_copy(attn_proj_hbm, aproj, weight_sem.at[1]),
    ]
    loads = [
        pltpu.make_async_copy(src, dst, load_sem.at[i])
        for i, (src, dst) in enumerate(
            (
                (segs_hbm, segs_ref.at[1 + side, 0]),
                (key_hbm.at[:, kv_cols], kv.at[me, 0, body]),
                (value_hbm.at[:, kv_cols], kv.at[me, 1, body]),
                (groups_hbm, g_in.at[side]),
                (taps_groups_hbm, taps_groups_ref),
                (inner_hbm.at[:, side_half(side)], x_in.at[side]),
                (taps_inner_hbm.at[:, side_half(side)], taps_inner_ref),
                (step_hbm, step_in.at[side]),
                (bias_hbm, bias_ref),
                (decay_hbm, decay_ref),
                (query_hbm, query_ref),
                (gate_hbm, gate_ref),
                (gain_hbm, gain_ref),
            )
        )
    ]

    barrier = pltpu.get_barrier_semaphore()

    def hello(target):
        pl.semaphore_signal(barrier, inc=1, device_id=target, device_id_type=MESH)

    hello(at_seq(partner))
    hello(at_head(sibling))
    hello(at_head(opposite))

    def hello_later(s, _):
        hello(at_seq(me + 2 * s))
        return 0

    lax.fori_loop(1, last_pair - pair + 1, hello_later, 0)

    @pl.when(has_upper & (side == 1))
    def _():
        hello(at_seq(following))

    for w in loads:
        w.start()
    pl.semaphore_wait(barrier, 3 + pair + jnp.where(has_lower, other, 0))

    def answer(k):
        pl.semaphore_signal(ready.at[me], inc=1, device_id=at_seq(k), device_id_type=MESH)

    @pl.when(has_lower & (side == 0))
    def _():
        answer(previous)

    lax.fori_loop(1, pair + 1, lambda s, _: answer(me - 2 * s) or 0, 0)

    tail_rows = pl.ds(tokens - RIM, RIM)

    def rim_copies(kind, target, slot, which):
        return [
            remote(
                inner_hbm.at[tail_rows, side_half(which)], rim_x.at[slot], rim_ss.at[kind, 0], rim_rs.at[slot, 0], at_seq(target)
            ),
            remote(groups_hbm.at[tail_rows, :], rim_g.at[slot], rim_ss.at[kind, 1], rim_rs.at[slot, 1], at_seq(target)),
        ]

    def rim_next():
        return rim_copies(0, following, other, other)

    def rim_skip():
        return rim_copies(1, upper, 0, side)

    def group_copy(block, kind):
        at = core_cols(kind)
        return remote(groups_hbm.at[:, at], g_in.at[block, :, at], g_ss.at[kind], g_rs.at[kind], at_seq(partner))

    def x_copy(block, c):
        return remote(
            inner_hbm.at[:, part(other, c)],
            x_in.at[block, :, pl.ds(c * LANES, LANES)],
            x_ss.at[c],
            x_rs.at[c],
            at_seq(partner),
        )

    def step_copy(block):
        return remote(step_hbm, step_in.at[block], step_sem.at[0], step_sem.at[1], at_seq(partner))

    def seg_copy(kind, target, dst):
        return remote(segs_hbm, segs_ref.at[dst, 0], seg_ss.at[kind], seg_rs.at[dst], at_seq(target))

    step_copy(side).start()
    seg_copy(0, partner, 1 + side).start()

    group_copy(side, 0).start()
    x_copy(side, 0).start()

    @pl.when(side == 0)
    def _():
        for c in rim_next():
            c.start()

    for c in range(1, chunks):
        x_copy(side, c).start()
    group_copy(side, 1).start()

    def kv_copy(b, k):
        return remote(kv.at[b, core], kv.at[b, core], kv_ss.at[k], kv_rs.at[b], at_seq(k))

    def kv_share(b):
        return remote(kv.at[b, core], kv.at[b, core], share_ss.at[b], share_rs.at[b], at_head(sibling))

    def kv_across(b):
        return remote(kv.at[b, core], kv.at[b, core], across_ss.at[b], kv_rs.at[b], at_seq(partner))

    def pass_on(s, _):
        kv_copy(me - 2 * s, partner).wait_recv()
        kv_across(me - 2 * s).start()
        kv_share(me - 2 * s).start()
        return 0

    def pass_across(s, _):
        kv_across(partner - 2 * s).wait_recv()
        kv_share(partner - 2 * s).start()
        return 0

    def conv_flags(b, before):
        now = segs_of(b + 1)
        both_blocks = jnp.concatenate([before, now], axis=1)
        row = iota((8, tokens), 0)
        flags = now
        for back in range(1, taps):
            kept = (pltpu.roll(both_blocks, back, 1)[:, tokens:] == now).astype(F32)
            flags = jnp.where(row == back, kept, flags)
        eye = (iota((8, 8), 0) == iota((8, 8), 1)).astype(BF16)
        return dot(flags.astype(BF16), eye, (0, 0))

    def keeps_of(flags, n):
        return [jnp.broadcast_to(flags[:n, back : back + 1], (n, LANES)) > 0.5 for back in range(taps - 1, 0, -1)]

    def conv(pad, b, cols, keeps, weight_ref, n):
        acc = weight_ref[taps - 1 : taps, cols] * pad[b, RIM : RIM + n, cols]
        for k in range(taps - 1):
            first = RIM - (taps - 1) + k
            term = weight_ref[k : k + 1, cols] * pad[b, first : first + n, cols]
            acc = acc + jnp.where(keeps[k], term, 0.0)
        return jax.nn.silu(acc).astype(BF16)

    def conv_groups(b, kind, keeps, n):
        out = (conv_b, conv_c)[kind]
        for c in range(0, STATE_SIZE, LANES):
            at = slice(kind * STATE_SIZE + c, kind * STATE_SIZE + c + LANES)
            out[b, 0:n, c : c + LANES] = conv(pad_g, b, at, keeps, taps_groups_ref, n)

    def conv_inner(b, c, keeps, n):
        at = slice(c * LANES, (c + 1) * LANES)
        conv_x[b, 0:n, at] = conv(pad_x, b, at, keeps, taps_inner_ref, n)

    def rim_arrived(slot):
        for c in rim_copies(0, partner, slot, slot):
            c.wait_recv()

    def segs_of(at):
        return jnp.broadcast_to(segs_ref[at].astype(F32), (8, tokens))

    for w in (loads[0], *loads[3:7]):
        w.wait()
    pad_g[side, 0:RIM, :] = jnp.zeros((RIM, wide), F32)
    pad_x[side, 0:RIM, :] = jnp.zeros((RIM, half), F32)
    pad_g[side, RIM:, :] = g_in[side].astype(F32)
    pad_x[side, RIM:, :] = x_in[side].astype(F32)
    own_flags = conv_flags(side, jnp.full((8, tokens), -1.0, F32))
    own_keeps = keeps_of(own_flags, tokens)
    conv_groups(side, 0, own_keeps, tokens)

    own_segs = jnp.broadcast_to(segs_ref[1 + side].astype(F32), (RIM, tokens)).astype(BF16)
    kv[me, 0, pl.ds(tokens, RIM), :] = own_segs
    kv[me, 1, pl.ds(tokens, RIM), :] = own_segs
    loads[1].wait()
    loads[2].wait()

    @pl.when(side == 0)
    def _():
        kv_across(me).start()

    @pl.when(has_upper)
    def _():
        pl.semaphore_wait(ready.at[upper], 1)

    @pl.when(has_upper & (side == 1))
    def _():
        pl.semaphore_wait(ready.at[following], 1)
        seg_copy(1, following, 0).start()
        seg_copy(2, upper, 0).start()
        for c in rim_skip():
            c.start()
        for c in rim_next():
            c.start()

    @pl.when(has_upper)
    def _():
        kv_copy(me, upper).start()

    for c in range(chunks):
        conv_inner(side, c, own_keeps, tokens)

    for w in loads[7:10]:
        w.wait()
    step_copy(other).wait_recv()
    seg_copy(0, partner, 1 + other).wait_recv()
    bias = column(bias_ref[...].reshape(1, heads))
    rates = jnp.exp(column(decay_ref[...].reshape(1, heads)))
    on_left = side == 0

    def mine_of(a):
        kept = jnp.where(on_left, a[:few], a[few:])
        return jnp.concatenate([kept, jnp.zeros((8 - few, a.shape[1]), F32)], axis=0)

    raw = mine_of(jnp.concatenate([step_in[0], step_in[1]], axis=1) + bias)
    steps = jnp.maximum(raw, 0.0) + jnp.log1p(jnp.exp(-jnp.abs(raw)))
    span = 2 * tokens
    row_t, col_t = iota((span, span), 0), iota((span, span), 1)
    upto = (row_t <= col_t).astype(BF16)
    sums = dot(thirds(-steps * mine_of(rates)), upto, (1, 0))
    cumul = sums[0:8] + sums[8:16] + sums[16:24]
    total = cumul[:, span - 1 : span]
    segs_rows8 = jnp.concatenate([segs_of(1), segs_of(2)], axis=1)
    last_seg = segs_rows8[:, span - 1 : span]
    weigh = jnp.where(segs_rows8 == last_seg, jnp.exp(total - cumul), 0.0) * steps
    cols = to_columns(jnp.concatenate([cumul, weigh, jnp.exp(cumul), segs_rows8], axis=0))
    left = iota((span, LANES), 1) < HEAD_CHANNELS

    def two_heads(base, c):
        a, b = base + 2 * c, base + 2 * c + 1
        return jnp.where(left, cols[:, a : a + 1], cols[:, b : b + 1])

    group_copy(other, 0).wait_recv()

    def send_far(s, _):
        pl.semaphore_wait(ready.at[me + 2 * s], 1)
        kv_copy(me, me + 2 * s).start()
        return 0

    lax.fori_loop(2, last_pair - pair + 1, send_far, 0)

    other_keeps = keeps_of(conv_flags(other, jnp.full((8, tokens), -1.0, F32)), tokens)
    pad_g[other, 0:RIM, :] = jnp.zeros((RIM, wide), F32)
    pad_x[other, 0:RIM, :] = jnp.zeros((RIM, half), F32)
    pad_g[other, RIM:, 0:STATE_SIZE] = g_in[other, :, 0:STATE_SIZE].astype(F32)
    conv_groups(other, 0, other_keeps, tokens)

    def conv_other(c):
        lanes = slice(c * LANES, (c + 1) * LANES)
        x_copy(other, c).wait_recv()
        pad_x[other, RIM:, lanes] = x_in[other, :, lanes].astype(F32)
        conv_inner(other, c, other_keeps, tokens)

    conv_other(0)

    @pl.when(has_lower)
    def _():
        seg_copy(0, partner, 0).wait_recv()
        rim_arrived(0)

    @pl.when(pair == 0)
    def _():
        segs_ref[0] = jnp.full((1, tokens), -1, jnp.int32)
        rim_x[0] = jnp.zeros_like(rim_x[0])
        rim_g[0] = jnp.zeros_like(rim_g[0])

    @pl.when(side == 1)
    def _():
        rim_arrived(1)

    @pl.when(side == 0)
    def _():
        rim_x[1] = x_in[0, tokens - RIM :, :]
        rim_g[1] = g_in[0, tokens - RIM :, :]

    first_keeps = []
    for b in range(2):
        pad_g[b, 0:RIM, :] = rim_g[b].astype(F32)
        pad_x[b, 0:RIM, :] = rim_x[b].astype(F32)
        first_keeps.append(keeps_of(conv_flags(b, segs_of(b)), RIM))
        conv_groups(b, 0, first_keeps[b], RIM)

    read_b = conv_b[...].reshape(span, STATE_SIZE)
    across_b = read_b.T

    def hop(src, dst, ss, rs, c, target):
        return remote(src.at[c], dst.at[c], ss.at[c], rs.at[c], at_seq(target))

    def e_hop(i, target):
        return hop(e_send, e_recv, e_ss, e_rs, i, target)

    for c in range(chunks):
        if c > 0:
            conv_other(c)
        for b in range(2):
            conv_inner(b, c, first_keeps[b], RIM)
        lanes = slice(c * LANES, (c + 1) * LANES)
        x = conv_x[:, :, lanes].reshape(span, LANES).astype(F32)
        state[:, lanes] = dot(across_b, (two_heads(8, c) * x).astype(BF16), (1, 0))

        @pl.when(pair == 0)
        def _():
            for r in range(PIECES):
                i = PIECES * c + r
                e_send[i] = state[r * depth : (r + 1) * depth, lanes].astype(BF16)
                e_hop(i, upper).start()

    lax.fori_loop(1, pair + 1, pass_on, 0)
    group_copy(other, 1).wait_recv()
    pad_g[side, 0:RIM, STATE_SIZE:] = jnp.zeros((RIM, STATE_SIZE), F32)
    conv_groups(side, 1, own_keeps, tokens)
    pad_g[side, 0:RIM, STATE_SIZE:] = rim_g[side, :, STATE_SIZE:].astype(F32)

    prev_last = segs_of(0)[:, tokens - 1 : tokens]
    spread = iota((8, half), 1) // HEAD_CHANNELS == iota((8, half), 0)
    crossing_pair = jnp.where(last_seg == prev_last, jnp.exp(total), 0.0)
    through = jnp.sum(jnp.where(spread, crossing_pair, 0.0), axis=0, keepdims=True)
    joined = cols[:, 24:25] == prev_last[0:1]
    pad_g[other, RIM:, STATE_SIZE:] = g_in[other, :, STATE_SIZE:].astype(F32)
    conv_groups(other, 1, other_keeps, tokens)
    for b in range(2):
        conv_groups(b, 1, first_keeps[b], RIM)
    read_c = conv_c[...].reshape(span, STATE_SIZE)

    for w in weights:
        w.start()

    for w in loads[10:]:
        w.wait()
    scale = 1.0 / math.sqrt(HD)
    queries = jnp.concatenate([query_ref[:, h * HD : (h + 1) * HD] for h in range(heads_here)], axis=0)
    rows = heads_here * tokens
    segs_q = jnp.concatenate([own_flags[:, 0:1]] * heads_here, axis=0)
    token_q = jnp.concatenate([iota((tokens, 1), 0)] * heads_here, axis=0)
    top_ref[...] = jnp.full((rows, tokens), -jnp.inf, F32)
    total_ref[...] = jnp.zeros((rows, tokens), F32)
    summed_ref[...] = jnp.zeros((rows, HD), F32)

    def attend(k):
        @pl.when(k != me)
        def _():
            kv_share(k).wait_recv()

        scores = dot(queries, kv[k, 0, 0:tokens, :], (1, 1)) * scale
        segs_k = kv[k, 0, tokens:, :].astype(F32)[0:1, :tokens]
        allowed = (segs_k == segs_q) & (iota((rows, tokens), 1) + (k - me) * tokens <= token_q)
        scores = jnp.where(allowed, scores, -jnp.inf)
        scores_ref[k] = scores
        top_ref[...] = jnp.maximum(top_ref[...], scores)

    same_head = (iota((2 * LANES, LANES), 0) % LANES // HEAD_CHANNELS == iota((2 * LANES, LANES), 1) // HEAD_CHANNELS).astype(
        BF16
    )
    gain_row = gain_ref[...].reshape(1, channels)
    gains = [
        jnp.where(on_left, gain_row[:, :half], gain_row[:, half:]),
        jnp.where(on_left, gain_row[:, half:], gain_row[:, :half]),
    ]

    def norm(which, c, gain, y):
        at = part(which, c)
        gated = y * jax.nn.silu(gate_ref[:, at].astype(F32))
        square = gated * gated
        high = square.astype(BF16)
        parts = jnp.concatenate([high, (square - high.astype(F32)).astype(BF16)], axis=1)
        mean_square = dot(parts, same_head, (1, 0)) * (1.0 / HEAD_CHANNELS)
        normed = gated * lax.rsqrt(mean_square + 1e-05) * gain[:, c * LANES : (c + 1) * LANES]
        both[:, at] = normed.astype(BF16)

    def f_hop(c):
        return hop(f_send, f_recv, f_ss, f_rs, c, partner)

    @pl.when(pair == 0)
    def _():
        e_recv[...] = jnp.zeros_like(e_recv)

    live = (cols[:, 24:25] == segs_rows8[0:1]) & (row_t >= col_t)
    crossing = dot(read_c, across_b, (1, 0))
    for c in range(chunks):
        lanes = slice(c * LANES, (c + 1) * LANES)
        x = conv_x[:, :, lanes].reshape(span, LANES)
        got = []
        for h in (2 * c, 2 * c + 1):
            halves = []
            for rows_of, width in ((slice(0, tokens), tokens), (slice(tokens, span), span)):
                gap = cols[rows_of, h : h + 1] - cumul[h : h + 1, :width]
                decays = jnp.exp(jnp.where(live[rows_of, :width], gap, -jnp.inf))
                mixing = (crossing[rows_of, :width] * decays * steps[h : h + 1, :width]).astype(BF16)
                halves.append(dot(mixing, x[:width], (1, 0)))
            got.append(jnp.concatenate(halves, axis=0))
        y_ref[:, lanes] = jnp.where(left, got[0], got[1])

    def attend_line():
        lax.fori_loop(0, pair + 1, lambda s, _: attend(me - 2 * s) or 0, 0)
        lax.fori_loop(other, pair + 1, pass_across, 0)

    def attend_rest():
        lax.fori_loop(other, pair + 1, lambda s, _: attend(partner - 2 * s) or 0, 0)
        top = jnp.max(top_ref[...], axis=1, keepdims=True)

        def add(k, _):
            w = jnp.exp(scores_ref[k] - top)
            total_ref[...] += w
            summed_ref[...] += dot(w.astype(BF16), kv[k, 1, 0:tokens, :], (1, 0))
            return 0

        lax.fori_loop(0, me + 1, add, 0)
        attended = (summed_ref[...] / jnp.sum(total_ref[...], axis=1, keepdims=True)).astype(BF16)
        for h in range(heads_here):
            both[:, channels + h * HD : channels + (h + 1) * HD] = attended[h * tokens : (h + 1) * tokens]

    pl.when(pair == last_pair)(attend_line)
    for c in range(chunks):
        lanes = slice(c * LANES, (c + 1) * LANES)

        @pl.when(has_lower)
        def _():
            for r in range(PIECES):
                i = PIECES * c + r
                e_hop(i, partner).wait_recv()

                @pl.when(has_upper)
                def _():
                    enters = e_recv[i].astype(F32)
                    e_send[i] = (through[:, lanes] * enters + state[r * depth : (r + 1) * depth, lanes]).astype(BF16)
                    e_hop(i, upper).start()

        enters = jnp.concatenate([e_recv[PIECES * c + r] for r in range(PIECES)], axis=0)
        carried = jnp.where(joined, two_heads(16, c), 0.0) * dot(read_c, enters, (1, 0))
        y = y_ref[:, lanes] + carried
        f_send[c] = jnp.where(on_left, y[tokens:], y[:tokens]).astype(BF16)
        f_hop(c).start()
        norm(side, c, gains[0], jnp.where(on_left, y[:tokens], y[tokens:]))

    pl.when(pair < last_pair)(attend_line)
    attend_rest()
    for c in range(chunks):
        f_hop(c).wait_recv()
        norm(other, c, gains[1], f_recv[c].astype(F32))

    for w in weights:
        w.wait()
    width = out_ref.shape[1]

    def product(j, part_of):
        at = pl.ds(pl.multiple_of(j * width + part_of * (width // CUTS), LANES), width // CUTS)
        return dot(both[:, :channels], mproj[:, at], (1, 0)) + dot(both[:, channels:], aproj[:, at], (1, 0))

    def rs_copy(i, target):
        return remote(rs_send.at[i], rs_recv.at[i], rs_ss.at[i], rs_rs.at[i], at_head(target))

    to_pair = [rs_copy(h, sibling) for h in range(CUTS)]
    to_sibling = [rs_copy(CUTS + h, sibling) for h in range(CUTS)]
    to_opposite = [rs_copy(2 * CUTS + h, opposite) for h in range(CUTS)]
    for h in range(CUTS):
        rs_send[h] = product(opposite_sibling, h).astype(BF16)
        to_pair[h].start()
    for h in range(CUTS):
        away = product(opposite, h)
        to_pair[h].wait_recv()
        rs_send[2 * CUTS + h] = (away + rs_recv[h].astype(F32)).astype(BF16)
        to_opposite[h].start()
    for h in range(CUTS):
        rs_send[CUTS + h] = product(sibling, h).astype(BF16)
        to_sibling[h].start()
    for h in range(CUTS):
        result = product(mine, h)
        to_sibling[h].wait_recv()
        result = result + rs_recv[CUTS + h].astype(F32)
        to_opposite[h].wait_recv()
        out_ref[:, h * (width // CUTS) : (h + 1) * (width // CUTS)] = (result + rs_recv[2 * CUTS + h].astype(F32)).astype(BF16)

    for copy in (*to_pair, *to_sibling, *to_opposite, step_copy(side)):
        copy.wait_send()
    for c in range(chunks):
        x_copy(side, c).wait_send()
        f_hop(c).wait_send()
    for kind in range(2):
        group_copy(side, kind).wait_send()
    seg_copy(0, partner, 1 + side).wait_send()

    @pl.when(me < n_seq - 1)
    def _():
        for c in rim_next():
            c.wait_send()

    @pl.when(has_upper & (side == 1))
    def _():
        for c in rim_skip():
            c.wait_send()
        seg_copy(1, following, 0).wait_send()
        seg_copy(2, upper, 0).wait_send()

    @pl.when(has_upper)
    def _():
        for i in range(PIECES * chunks):
            e_hop(i, upper).wait_send()

    def sent_kv(s, _):
        kv_copy(me, me + 2 * s).wait_send()
        return 0

    lax.fori_loop(1, last_pair - pair + 1, sent_kv, 0)

    def sent_on(s, _):
        kv_across(me - 2 * s).wait_send()
        kv_share(me - 2 * s).wait_send()
        return 0

    lax.fori_loop(1, pair + 1, sent_on, 0)

    @pl.when(side == 0)
    def _():
        kv_across(me).wait_send()

    def sent_share(s, _):
        kv_share(partner - 2 * s).wait_send()
        return 0

    lax.fori_loop(other, pair + 1, sent_share, 0)


def shards(n_seq, n_head, *arrays):
    (inner, groups, gate, step, bias, decay, taps_i, taps_g, gain, query, key, value, segs, mproj, aproj) = arrays
    tokens, channels = inner.shape
    half = channels // 2
    wide = groups.shape[1]
    out_width = mproj.shape[1] // n_head
    chunks = half // LANES
    vmem = pl.BlockSpec(memory_space=pltpu.VMEM)
    hbm = pl.BlockSpec(memory_space=pltpu.HBM)
    dma = pltpu.SemaphoreType.DMA
    scratch = [
        pltpu.VMEM((3, 1, tokens), segs.dtype),
        pltpu.VMEM((2, *step.shape), F32),
        pltpu.VMEM(bias.shape, F32),
        pltpu.VMEM(decay.shape, F32),
        pltpu.VMEM((taps_i.shape[0], half), F32),
        pltpu.VMEM(taps_g.shape, F32),
        pltpu.VMEM(gain.shape, F32),
        pltpu.VMEM(query.shape, BF16),
        pltpu.VMEM(gate.shape, BF16),
        pltpu.VMEM((2, tokens, half), BF16),
        pltpu.VMEM((2, tokens, wide), BF16),
        pltpu.VMEM((2, RIM, half), BF16),
        pltpu.VMEM((2, RIM, wide), BF16),
        pltpu.VMEM((n_seq, 2, tokens + RIM, HD), BF16),
        pltpu.VMEM((2, RIM + tokens, half), F32),
        pltpu.VMEM((2, RIM + tokens, wide), F32),
        pltpu.VMEM((2, tokens, half), BF16),
        pltpu.VMEM((2, tokens, STATE_SIZE), BF16),
        pltpu.VMEM((2, tokens, STATE_SIZE), BF16),
        pltpu.VMEM((2 * tokens, half), F32),
        pltpu.VMEM((STATE_SIZE, half), F32),
        *[pltpu.VMEM((PIECES * chunks, STATE_SIZE // PIECES, LANES), BF16) for _ in range(2)],
        *[pltpu.VMEM((chunks, tokens, LANES), BF16) for _ in range(2)],
        pltpu.VMEM((tokens, channels + query.shape[1]), BF16),
        pltpu.VMEM(mproj.shape, BF16),
        pltpu.VMEM(aproj.shape, BF16),
        pltpu.VMEM((3 * CUTS, tokens, out_width // CUTS), BF16),
        pltpu.VMEM((3 * CUTS, tokens, out_width // CUTS), BF16),
        pltpu.VMEM((n_seq, query.shape[1] // HD * tokens, tokens), F32),
        *[pltpu.VMEM((query.shape[1] // HD * tokens, n), F32) for n in (tokens, tokens, HD)],
        pltpu.SemaphoreType.REGULAR((n_seq,)),
        dma((13,)),
        dma((2,)),
        dma((chunks,)),
        dma((chunks,)),
        dma((2,)),
        dma((2,)),
        dma((2,)),
        dma((2, 2)),
        dma((2, 2)),
        dma((3,)),
        dma((3,)),
        *[dma((n_seq,)) for _ in range(5)],
        *[dma((PIECES * chunks,)) for _ in range(2)],
        *[dma((chunks,)) for _ in range(2)],
        dma((3 * CUTS,)),
        dma((3 * CUTS,)),
    ]
    return pl.pallas_call(
        functools.partial(kernel, n_seq, n_head),
        out_shape=jax.ShapeDtypeStruct((tokens, out_width), BF16),
        in_specs=[hbm] * 15,
        out_specs=vmem,
        scratch_shapes=scratch,
        compiler_params=pltpu.CompilerParams(
            collective_id=0, has_side_effects=True, vmem_limit_bytes=64 * 2**20
        ),
        name="mixer",
    )(*arrays)


def solution(mesh):
    placed = (
        P("seq", "head"),
        P("seq", None),
        P("seq", "head"),
        P("head", "seq"),
        P("head"),
        P("head"),
        P(None, "head"),
        P(),
        P("head"),
        P("seq", "head"),
        P("seq", None),
        P("seq", None),
        P("seq"),
        P("head", None),
        P("head", None),
    )
    return jax.shard_map(
        functools.partial(shards, mesh.shape["seq"], mesh.shape["head"]),
        mesh=mesh,
        in_specs=placed,
        out_specs=P("seq", "head"),
        check_vma=False,
    )
```
